32 devices in a mesh: section: 8 (over z, y), dp: 4 (over x, core).
Axes of the slice: x: 2, y: 2, z: 4, core: 2. Of those that a mesh axis runs over, the one named last changes fastest.
Arguments:
- entering: bfloat16 [8, 512, 8192], P('section', 'dp'), may hold values from -6 to 6
- returning: bfloat16 [8, 512, 8192], P('section', 'dp'), may hold values from -6 to 6
- adapter_down: bfloat16 [2, 8, 64, 8192], P(None, 'section'), may hold values from -0.0625 to 0.0625
- adapter_up: bfloat16 [2, 8, 64, 8192], P(None, 'section'), may hold values from -0.75 to 0.75
- stashed: float32 [8, 3, 64, 512], P('section', None, None, 'dp'), may hold values from -6 to 6
- doc_ids: int32 [8, 512], P(None, 'dp'), may hold values from 0 to 7, never falling along the last dimension, each value on 1 to 256 neighbouring positions
- input_factor: float32 [8, 8192, 1024], P('section', 'dp'), may hold values from -3 to 3
- output_factor: float32 [2, 8, 64, 64], P(None, 'section'), may hold values from -3 to 3
Outputs:
- input_factor_new: float32 [8, 8192, 1024], P('section', 'dp')
- output_factor_new: float32 [2, 8, 64, 64], P(None, 'section')
The draws below stay inside these ranges and needn't reach their ends.
Inputs may be any that keep to these rules, and one draw needn't show every extreme that they name: `doc_ids`: each row packs 8 documents in order: document numbers never fall along a row, every document has 1 to 256 tokens, and some document of every row has exactly 256.
All inputs are finite; a program needn't handle non-finite values.
Results may differ from the reference program's by a relative error of at most 0.0044.
Values may be sent and summed in bfloat16 or wider, within the bound.
A program may use at most 128 MiB of HBM per device.

```python
import math
import jax
import jax.numpy as jnp
import numpy as np
from jax import lax

D = 8192
R = 64
BLK = 1024
TOK = 128
STEPS = 3
SECTIONS = 8
TOKENS = 512
DOCS = 8
DOC_MAX = 256
N_DP = 4


def block_levels(rng, shape, cuts, low, top_value):
    def one(axis_at, shards_of):
        heights = jax.random.uniform(jax.random.fold_in(jax.random.fold_in(rng, 6), axis_at), (shards_of,), jnp.float32, low / len(cuts), top_value / len(cuts))
        return jnp.repeat(jnp.exp(heights), shape[axis_at] // shards_of).reshape((-1,) + (1,) * (len(shape) - axis_at - 1))

    factor_of = one(*cuts[0])
    for cut in cuts[1:]:
        factor_of = factor_of * one(*cut)
    return factor_of


def split_up(count, total, limit, slope):
    loads = [(1 << 20) // math.isqrt(grade ** slope) + 1 for grade in range(2, count + 1)]
    spare, given = total - limit - (count - 1), [1] * (count - 1)
    while spare > 0:
        candidates = [i for i in range(count - 1) if given[i] < limit]
        mass, remaining = sum([loads[i] for i in candidates]), spare
        for i in candidates:
            addition = min(limit - given[i], max(1, remaining * loads[i] // mass), spare)
            given[i] = given[i] + addition
            spare = spare - addition
    return np.array([limit] + given)


def ragged(own_key, number_of, total, reach, slope):
    if number_of == 2:
        one = jax.random.randint(own_key, (), max(1, total - reach), min(reach, total - 1) + 1)
        return jnp.stack([one, total - one])
    lengths = jnp.asarray(split_up(number_of, total, reach, slope), jnp.int32)
    pairs = (number_of - 1) // 2
    donor, receiver = lengths[1:1 + 2 * pairs:2], lengths[2:2 + 2 * pairs:2]
    margin = jnp.minimum(donor - 1, reach - receiver)
    moved = jax.random.randint(jax.random.fold_in(own_key, 1), (pairs,), 0, 1 << 20) % (margin + 1)
    lengths = lengths.at[1:1 + 2 * pairs:2].set(donor - moved).at[2:2 + 2 * pairs:2].set(receiver + moved)
    return lengths[jax.random.permutation(jax.random.fold_in(own_key, 2), number_of)]


def bell_draw(key, extent, width, reach, pieces=(), kind=jnp.bfloat16):
    level = block_levels(key, extent, pieces, -0.22, 0.18) if pieces else 1.0
    result = jax.random.normal(key, extent, jnp.float32) * width * level
    return jnp.minimum(jnp.maximum(result, -reach), reach).astype(kind)


def setup_inputs(seed: int = 0) -> dict:
    splits = jax.random.split(jax.random.key(seed), 9)
    entering = bell_draw(splits[0], (SECTIONS, TOKENS, D), 1.0, 6.0, ((0, 8), (1, 4)))
    returning = bell_draw(splits[1], (SECTIONS, TOKENS, D), 1.0, 6.0, ((0, 8), (1, 4)))
    adapter_down = bell_draw(splits[2], (2, SECTIONS, R, D), D ** -0.5, 0.0625, ((1, 8),))
    adapter_up = bell_draw(splits[3], (2, SECTIONS, R, D), R ** -0.5, 0.75, ((1, 8),))
    stashed = bell_draw(splits[4], (SECTIONS, STEPS, R, TOKENS), 1.5, 6.0, ((0, 8), (3, 4)), jnp.float32)
    doc_ids = jax.vmap(lambda own: jnp.searchsorted(jnp.cumsum(ragged(own, DOCS, TOKENS, DOC_MAX, 2)), jnp.arange(TOKENS), side="right"))(jax.random.split(splits[5], SECTIONS)).reshape((SECTIONS, TOKENS)).astype(jnp.int32)
    input_factor = bell_draw(splits[6], (SECTIONS, D, BLK), 0.5, 3.0, ((0, 8), (1, 4)), jnp.float32)
    output_factor = bell_draw(splits[7], (2, SECTIONS, R, R), 0.5, 3.0, ((1, 8),), jnp.float32)
    return {"entering": entering, "returning": returning, "adapter_down": adapter_down, "adapter_up": adapter_up, "stashed": stashed, "doc_ids": doc_ids, "input_factor": input_factor, "output_factor": output_factor}


def layer_apply(current, down_proj, up_proj):
    pre_act = jnp.dot(current, down_proj.T, preferred_element_type=jnp.float32)
    gated = jax.nn.silu(pre_act).astype(jnp.bfloat16)
    mixed = jnp.dot(gated, up_proj, preferred_element_type=jnp.float32)
    return (current.astype(jnp.float32) + mixed).astype(jnp.bfloat16)

def replica_part(carry, replica_rows):
    grouped = replica_rows.astype(jnp.float32).reshape(replica_rows.shape[0], D // BLK, BLK)
    product = jnp.einsum('tki,tkj->kij', grouped, grouped, precision=lax.Precision.HIGHEST)
    rounded = lax.optimization_barrier(product.reshape(D, BLK).astype(jnp.bfloat16))
    return (carry + rounded.astype(jnp.float32), None)

def reference(entering, returning, adapter_down, adapter_up, stashed, doc_ids, input_factor, output_factor):
    section_count = SECTIONS
    doc_range = jnp.arange(DOCS, dtype=jnp.int32)
    onehot = (doc_ids[:, :, None] == doc_range[None, None, :]).astype(jnp.float32)
    counts = lax.optimization_barrier(jnp.sum(onehot, axis=1))
    doc_length = lax.optimization_barrier(jnp.sum(onehot * counts[:, None, :], axis=2))
    weight = jnp.sqrt(TOK / doc_length)
    first = [1 if anchor < section_count // 2 else 0 for anchor in range(section_count)]
    current = [entering[section_idx] for section_idx in range(section_count)]
    row_lists = [[] for section_idx in range(section_count)]
    for step_idx in range(STEPS):
        advanced = []
        for section_idx in range(section_count):
            anchor = (section_idx - step_idx) % section_count
            span_id = first[anchor] + (1 if section_idx < step_idx else 0)
            scaled = jnp.sqrt(weight[anchor])[:, None] * current[section_idx].astype(jnp.float32)
            row_lists[section_idx].append(scaled.astype(jnp.bfloat16))
            if step_idx + 1 < STEPS:
                advanced.append(layer_apply(current[section_idx], adapter_down[span_id, section_idx], adapter_up[span_id, section_idx]))
        if step_idx + 1 < STEPS:
            current = [advanced[(section_idx - 1) % section_count] for section_idx in range(section_count)]
    new_blocks = []
    for section_idx in range(section_count):
        stacked = jnp.stack(row_lists[section_idx])
        held = stacked.shape[0]
        by_replica = jnp.transpose(stacked.reshape(held, N_DP, TOK, D), (1, 0, 2, 3)).reshape(N_DP, held * TOK, D)
        summed, _ = lax.scan(replica_part, jnp.zeros((D, BLK), jnp.float32), by_replica)
        new_blocks.append(0.75 * input_factor[section_idx] + 0.25 * summed / (STEPS * TOKENS))
    input_factor_new = jnp.stack(new_blocks)
    gradient = [returning[section_idx] for section_idx in range(section_count)]
    curv_sums = [[jnp.zeros((R, R), jnp.float32) for section_idx in range(section_count)] for span_idx in range(2)]
    step_counts = [[0 for section_idx in range(section_count)] for span_idx in range(2)]
    for step_idx in range(STEPS):
        passed = []
        for section_idx in range(section_count):
            span_id = 1 if section_idx + step_idx < section_count else 0
            stash_now = stashed[section_idx, step_idx].T
            grad_act = jnp.dot(gradient[section_idx], adapter_up[span_id, section_idx].T, preferred_element_type=jnp.float32)
            sigmoid_z = jax.nn.sigmoid(stash_now)
            grad_pre = (grad_act * sigmoid_z * (1.0 + stash_now * (1.0 - sigmoid_z))).astype(jnp.bfloat16)
            curv_sums[span_id][section_idx] = curv_sums[span_id][section_idx] + jnp.dot(grad_pre.T, grad_pre, preferred_element_type=jnp.float32)
            step_counts[span_id][section_idx] += 1
            if step_idx + 1 < STEPS:
                branch = jnp.dot(grad_pre, adapter_down[span_id, section_idx], preferred_element_type=jnp.float32)
                passed.append((gradient[section_idx].astype(jnp.float32) + branch).astype(jnp.bfloat16))
        if step_idx + 1 < STEPS:
            gradient = [passed[(section_idx + 1) % section_count] for section_idx in range(section_count)]
    span_rows = []
    for span_idx in range(2):
        section_rows = []
        for section_idx in range(section_count):
            held = step_counts[span_idx][section_idx]
            if held > 0:
                section_rows.append(0.75 * output_factor[span_idx, section_idx] + 0.25 * curv_sums[span_idx][section_idx] / (held * TOKENS))
            else:
                section_rows.append(output_factor[span_idx, section_idx])
        span_rows.append(jnp.stack(section_rows))
    output_factor_new = jnp.stack(span_rows)
    return (input_factor_new, output_factor_new)
```

```python
import functools

import jax
import jax.numpy as jnp
from jax import lax
from jax.experimental import pallas as pl
from jax.experimental.pallas import tpu as pltpu
from jax.sharding import PartitionSpec as P

BF16 = jnp.bfloat16
F32 = jnp.float32
ACROSS = (((1,), (1,)), ((), ()))
DOWNWARD = (((0,), (0,)), ((), ()))


def dot_nt(a, b):
    return lax.dot_general(a, b, ACROSS, preferred_element_type=F32)


def dot_nn(a, b):
    return jnp.dot(a, b, preferred_element_type=F32)


def long_dot(a_ref, b_ref, tile):
    width = a_ref.shape[-1]
    total = dot_nt(a_ref[:, 0:tile], b_ref[:, 0:tile])
    for at in range(tile, width, tile):
        total = total + dot_nt(a_ref[:, at : at + tile], b_ref[:, at : at + tile])
    return total


def split_dot_left(wide, narrow):
    high = wide.astype(BF16)
    low = (wide - high.astype(F32)).astype(BF16)
    return dot_nn(high, narrow) + dot_nn(low, narrow)


def split_dot_right(narrow, wide):
    high = wide.astype(BF16)
    low = (wide - high.astype(F32)).astype(BF16)
    return dot_nn(narrow, high) + dot_nn(narrow, low)


def forward_spans(anchor, n):
    first = 1 - anchor // (n // 2)
    return first, first + (anchor + 1) // n


def backward_span(anchor, step, n):
    section = (anchor - step + n) % n
    return 1 - (section + step) // n


def exchange_kernel(
    n, reps, parts,
    ent, ret, down, up, stash, docs,
    buf, upbuf, gbuf, docbuf, cbuf,
    ent_v, ret_v, down_v, up_v, stash_v, wfull, gsrc, msrc, mbuf, csrc,
    local_sem, send_sem, recv_sem,
):
    s = lax.axis_index("section")
    r = lax.axis_index("dp")
    chips = reps // 2
    chip, core = r // 2, r % 2
    tok, width = ent.shape
    rank = up.shape[1]
    share = width // reps
    wide = buf.shape[-1]
    tile = min(2048, width)

    def sec(shift):
        return (s + shift + n) % n

    def rep(dc, e):
        return ((chip + dc + chips) % chips) * 2 + (core + e) % 2

    def cols(replica):
        return pl.ds(pl.multiple_of(replica * share // wide * wide, 128), wide)

    def piece(replica):
        return pl.ds(pl.multiple_of(replica * share, 128), share)

    inner = pl.ds(pl.multiple_of(r * share % wide, 128), share)
    slots = [(d // 2, d % 2) for d in range(reps)]
    counts = {"copy": 0, "local": 0}
    copies = []
    locals_ = []

    def send(src, dst, section, replica):
        at = counts["copy"]
        counts["copy"] += 1
        copy = pltpu.make_async_remote_copy(
            src_ref=src, dst_ref=dst, send_sem=send_sem.at[at], recv_sem=recv_sem.at[at],
            device_id=(section, replica), device_id_type=pl.DeviceIdType.MESH,
        )
        copy.start()
        copies.append(copy)
        return copy

    def keep(src, dst):
        at = counts["local"]
        counts["local"] += 1
        copy = pltpu.make_async_copy(src, dst, local_sem.at[at])
        copy.start()
        return copy

    load_ent = keep(ent, ent_v)
    load_down = keep(down, down_v)
    load_up = keep(up, up_v)
    load_ret = keep(ret, ret_v)
    load_stash = keep(stash.at[0], stash_v.at[0])
    own_chunk = keep(ent.at[:, cols(r)], buf.at[0, 0])
    own_up = keep(up.at[:, :, cols(r)], upbuf.at[0])
    own_docs = keep(docs, docbuf.at[0])

    barrier = pltpu.get_barrier_semaphore()
    peers = 0
    for shift in (0, 1, 2, -1, -2):
        for dc, e in slots:
            if shift == 0 and dc == 0 and e == 0:
                continue
            pl.semaphore_signal(
                barrier, inc=1, device_id=(sec(shift), rep(dc, e)),
                device_id_type=pl.DeviceIdType.MESH,
            )
            peers += 1
    pl.semaphore_wait(barrier, peers)

    prev = sec(-1)
    w1_piece = send(
        down.at[forward_spans(prev, n)[1], :, piece(r)], wfull.at[0, :, piece(r)], prev, r
    )
    ups2 = send(up.at[:, :, cols(r)], upbuf.at[2], sec(2), r)
    st1 = send(stash.at[1], stash_v.at[1], sec(1), r)
    st2 = send(stash.at[2], stash_v.at[2], sec(2), r)
    inside = {}
    for dc, e in slots[1:]:
        target = rep(dc, e)
        inside[dc, e] = send(ent.at[:, cols(target)], buf.at[0, dc * 2 + e], s, target)
    doc_copies = [send(docs, docbuf.at[dc * 2 + e], s, rep(dc, e)) for dc, e in slots[1:]]

    half = tok // parts
    bands = [pl.ds(b * half, half) for b in range(parts)]
    ahead = {}

    def send_ahead(d):
        for b in range(parts):
            ahead[d, b] = send(buf.at[0, d, bands[b]], buf.at[2, d, bands[b]], sec(2), r)

    odd = s % 2
    partner = s + 1 - 2 * odd
    across = {}

    def send_across(d, b):
        ahead[d, b].wait_recv()
        across[d, b] = send(
            buf.at[2 * odd, d, bands[b]], buf.at[1, d, bands[b]], partner, r
        )

    own_chunk.wait()
    send_ahead(0)

    c0, _ = forward_spans(s, n)
    load_ent.wait()
    load_down.wait()
    z0 = long_dot(ent_v, down_v.at[c0], tile)
    g0 = (z0 / (1.0 + jnp.exp(-z0))).astype(BF16)
    gsrc[:, 0:rank] = g0

    inside[0, 1].wait_recv()
    send_ahead(1)

    def gather_start(which, own_ref):
        mine = wfull.at[which, :, piece(r)]
        out = {0: send(own_ref, mine, s, rep(0, 1))}
        for dc in range(1, chips):
            out[dc] = send(own_ref, mine, s, rep(dc, 0))
        return out

    def gather_pass(which, out):
        passed = []
        for dc in range(1, chips):
            out[dc].wait_recv()
            theirs = wfull.at[which, :, piece(rep(-dc, 0))]
            passed.append(send(theirs, theirs, s, rep(0, 1)))
        return passed

    def gather_end(out, passed):
        out[0].wait_recv()
        for copy in passed:
            copy.wait_recv()

    w1_piece.wait_recv()
    w1_out = gather_start(0, wfull.at[0, :, piece(r)])

    own_up.wait()
    ups2.wait_recv()
    ups1 = send(upbuf.at[2 * odd], upbuf.at[1], partner, r)
    span2 = backward_span(s, 2, n)
    own3 = keep(upbuf.at[2, span2, :, inner], wfull.at[2, :, piece(r)])
    w3_out = gather_start(2, upbuf.at[2, span2, :, inner])

    send_across_done = 0
    for d in range(2, reps):
        inside[slots[d]].wait_recv()
        send_ahead(d)
        if d == 2:
            w1_pass = gather_pass(0, w1_out)
            for b in range(parts):
                send_across(0, b)
            send_across_done = 1

    ups1.wait_recv()
    span1 = backward_span(s, 1, n)
    own2 = keep(upbuf.at[1, span1, :, inner], wfull.at[1, :, piece(r)])
    w2_out = gather_start(1, upbuf.at[1, span1, :, inner])
    w3_pass = gather_pass(2, w3_out)

    load_up.wait()
    gather_end(w1_out, w1_pass)
    p01 = long_dot(up_v.at[c0], wfull.at[0], tile)
    z1 = long_dot(ent_v, wfull.at[0], tile) + split_dot_right(g0, p01)
    gsrc[:, rank : 2 * rank] = (z1 / (1.0 + jnp.exp(-z1))).astype(BF16)
    g_copies = []
    for shift in (1, 2):
        for dc, e in slots:
            g_copies.append(send(gsrc, gbuf.at[shift - 1, dc * 2 + e], sec(shift), rep(dc, e)))

    after = sec(1)
    late2, late1 = backward_span(after, 2, n), backward_span(after, 1, n)
    keep(upbuf.at[1, late2, :, inner], msrc.at[0]).wait()
    keep(down.at[late1, :, piece(r)], msrc.at[1]).wait()
    mbuf[reps] = dot_nt(msrc[0], msrc[1])
    m_copies = []
    for dc, e in slots:
        m_copies.append(send(mbuf.at[reps], mbuf.at[dc * 2 + e], after, rep(dc, e)))

    for b in range(parts):
        send_across(1, b)
    w2_pass = gather_pass(1, w2_out)

    def gate(q):
        sigma = 1.0 / (1.0 + jnp.exp(-q))
        return sigma * (1.0 + q * (1.0 - sigma))

    load_ret.wait()
    load_stash.wait()
    a0 = long_dot(up_v.at[1], ret_v, tile)
    dz0 = (a0 * gate(stash_v[0])).astype(BF16)
    csrc[0] = dot_nt(dz0, dz0)
    gather_end(w3_out, w3_pass)
    own3.wait()
    n2 = long_dot(wfull.at[2], down_v.at[1], tile)
    a2 = long_dot(wfull.at[2], ret_v, tile) + split_dot_left(n2, dz0)
    gather_end(w2_out, w2_pass)
    own2.wait()
    n1 = long_dot(wfull.at[1], down_v.at[1], tile)
    a1 = long_dot(wfull.at[1], ret_v, tile) + split_dot_left(n1, dz0)
    st1.wait_recv()
    dz1 = (a1 * gate(stash_v[1])).astype(BF16)
    csrc[1] = dot_nt(dz1, dz1)
    for d in range(2, reps - 1):
        for b in range(parts):
            send_across(d, b)
    for copy in m_copies:
        copy.wait_recv()
    n3 = mbuf[0]
    for d in range(1, reps):
        n3 = n3 + mbuf[d]
    a2 = a2 + split_dot_left(n3, dz1)
    st2.wait_recv()
    dz2 = (a2 * gate(stash_v[2])).astype(BF16)
    csrc[2] = dot_nt(dz2, dz2)
    own_c = keep(csrc.at[0], cbuf.at[0, 0])
    c_copies = []
    for step in range(3):
        for dc, e in slots:
            if step == 0 and dc == 0 and e == 0:
                continue
            c_copies.append(
                send(csrc.at[step], cbuf.at[step, dc * 2 + e], sec(-step), rep(dc, e))
            )
    for b in range(parts):
        send_across(reps - 1, b)

    own_docs.wait()
    own_c.wait()
    for copy in doc_copies + g_copies + c_copies:
        copy.wait_recv()
    for copy in across.values():
        copy.wait_recv()
    for copy in copies:
        copy.wait_send()
    assert counts["copy"] <= send_sem.shape[0] and counts["local"] <= local_sem.shape[0]


def exchange(ent, ret, down, up, stash, docs, n, reps, wide, parts):
    tok, width = ent.shape
    rank = up.shape[1]
    slots = 140 if reps <= 4 else 60 * reps
    anywhere = pl.BlockSpec(memory_space=pl.ANY)
    return pl.pallas_call(
        functools.partial(exchange_kernel, n, reps, parts),
        out_shape=(
            jax.ShapeDtypeStruct((3, reps, tok, wide), BF16),
            jax.ShapeDtypeStruct((3, 2, rank, wide), BF16),
            jax.ShapeDtypeStruct((2, reps, tok, 2 * rank), BF16),
            jax.ShapeDtypeStruct((reps,) + docs.shape, jnp.int32),
            jax.ShapeDtypeStruct((3, reps, rank, rank), F32),
        ),
        in_specs=[anywhere] * 6,
        out_specs=(anywhere,) * 5,
        scratch_shapes=[
            pltpu.VMEM((tok, width), BF16),
            pltpu.VMEM((tok, width), BF16),
            pltpu.VMEM((2, rank, width), BF16),
            pltpu.VMEM((2, rank, width), BF16),
            pltpu.VMEM((3, rank, tok), F32),
            pltpu.VMEM((3, rank, width), BF16),
            pltpu.VMEM((tok, 2 * rank), BF16),
            pltpu.VMEM((2, rank, width // reps), BF16),
            pltpu.VMEM((reps + 1, rank, rank), F32),
            pltpu.VMEM((3, rank, rank), F32),
            pltpu.SemaphoreType.DMA((16,)),
            pltpu.SemaphoreType.DMA((slots,)),
            pltpu.SemaphoreType.DMA((slots,)),
        ],
        compiler_params=pltpu.CompilerParams(
            collective_id=0, has_side_effects=True, vmem_limit_bytes=40 * 1024 * 1024
        ),
        name="exchange",
    )(ent, ret, down, up, stash, docs)


def factor_kernel(n, reps, scale, buf, upbuf, gbuf, weight, old, new, rows):
    s = lax.axis_index("section")
    r = lax.axis_index("dp")
    step = pl.program_id(0)
    _, tokens, wide = buf.shape
    rank = upbuf.shape[2]
    height, block = old.shape
    share = height * pl.num_programs(0)

    @pl.when(step == 0)
    def _():
        piece = min(512, wide)
        back1, back2 = (s - 1 + n) % n, (s - 2 + n) % n
        first1, _ = forward_spans(back1, n)
        first2, second2 = forward_spans(back2, n)

        def fill(at, carry):
            here = pl.ds(pl.multiple_of(at * piece, piece), piece)
            rows[0:tokens, here] = (weight[0] * buf[0, :, here].astype(F32)).astype(BF16)
            act = buf[1, :, here].astype(F32) + dot_nn(
                gbuf[0, :, 0:rank], upbuf[1, first1, :, here]
            )
            act = act.astype(BF16).astype(F32)
            rows[tokens : 2 * tokens, here] = (weight[1] * act).astype(BF16)
            act = buf[2, :, here].astype(F32) + dot_nn(
                gbuf[1, :, 0:rank], upbuf[2, first2, :, here]
            )
            act = act.astype(BF16).astype(F32) + dot_nn(
                gbuf[1, :, rank : 2 * rank], upbuf[1, second2, :, here]
            )
            act = act.astype(BF16).astype(F32)
            rows[2 * tokens : 3 * tokens, here] = (weight[2] * act).astype(BF16)
            return carry

        lax.fori_loop(0, wide // piece, fill, 0)

    width = share * reps
    inside = (r * (width // reps)) % wide if width // reps < wide else 0
    left = pl.multiple_of(inside + step * height, 128)
    right = pl.multiple_of(left // block * block, block)
    total = lax.dot_general(
        rows[:, pl.ds(left, height)], rows[:, pl.ds(right, block)], DOWNWARD,
        preferred_element_type=F32,
    )
    new[...] = 0.75 * old[...] + total * scale


def update_factor(buf, upbuf, gbuf, weight, old, n, reps):
    share, block = old.shape
    _, tokens, wide = buf.shape
    height = min(256, share)
    whole = pl.BlockSpec(memory_space=pltpu.VMEM)
    tile = pl.BlockSpec((height, block), lambda i: (i, 0))
    return pl.pallas_call(
        functools.partial(factor_kernel, n, reps, 0.25 / (3 * tokens)),
        out_shape=jax.ShapeDtypeStruct(old.shape, F32),
        grid=(share // height,),
        in_specs=[whole, whole, whole, whole, tile],
        out_specs=tile,
        scratch_shapes=[pltpu.VMEM((3 * tokens, wide), BF16)],
        compiler_params=pltpu.CompilerParams(vmem_limit_bytes=56 * 1024 * 1024),
        name="factor",
    )(buf, upbuf, gbuf, weight, old)


def shards(
    entering, returning, adapter_down, adapter_up, stashed, doc_ids, input_factor, output_factor
):
    s = lax.axis_index("section")
    n = lax.axis_size("section")
    reps = lax.axis_size("dp")
    tok, width = entering.shape[1:]
    block = input_factor.shape[2]
    steps = stashed.shape[1]
    rank = stashed.shape[2]
    tokens = tok * reps
    wide = max(block, width // reps)
    buf, upbuf, gbuf, docbuf, cbuf = exchange(
        entering[0], returning[0], adapter_down[:, 0], adapter_up[:, 0], stashed[0], doc_ids,
        n, reps, wide, 2,
    )
    anchors = (s - jnp.arange(steps, dtype=jnp.int32)) % n
    mine = jnp.take(docbuf, anchors, axis=1).transpose(1, 0, 2).reshape(steps, tokens)
    same = mine[:, :, None] == jnp.arange(2 * reps, dtype=jnp.int32)
    counts = jnp.sum(same.astype(F32), axis=1)
    length = jnp.sum(jnp.where(same, counts[:, None, :], 0.0), axis=2)
    weight = jnp.sqrt(jnp.sqrt(tok / length))[:, :, None]
    factor = update_factor(
        buf.reshape(steps, tokens, wide), upbuf, gbuf.reshape(2, tokens, 2 * rank), weight,
        input_factor[0], n, reps,
    )
    curv = jnp.sum(cbuf, axis=1)
    second = (s + jnp.arange(steps) < n).astype(F32)
    member = jnp.stack([1.0 - second, second])
    held = jnp.sum(member, axis=1)
    total = jnp.sum(member[:, :, None, None] * curv[None], axis=1)
    divisor = (jnp.maximum(held, 1.0) * tokens)[:, None, None]
    updated = 0.75 * output_factor[:, 0] + 0.25 * total / divisor
    outer = jnp.where((held > 0.0)[:, None, None], updated, output_factor[:, 0])
    return factor[None], outer[:, None]


def solution(mesh):
    in_specs = (
        P("section", "dp", None),
        P("section", "dp", None),
        P(None, "section", None, None),
        P(None, "section", None, None),
        P("section", None, None, "dp"),
        P(None, "dp"),
        P("section", "dp", None),
        P(None, "section", None, None),
    )
    out_specs = (P("section", "dp", None), P(None, "section", None, None))
    return jax.shard_map(shards, mesh=mesh, in_specs=in_specs, out_specs=out_specs, check_vma=False)
```

```python
import functools

import jax
import jax.numpy as jnp
from jax import lax
from jax.experimental import pallas as pl
from jax.experimental.pallas import tpu as pltpu
from jax.sharding import PartitionSpec as P

BF16 = jnp.bfloat16
F32 = jnp.float32
ACROSS = (((1,), (1,)), ((), ()))
DOWNWARD = (((0,), (0,)), ((), ()))


def dot_nt(a, b):
    return lax.dot_general(a, b, ACROSS, preferred_element_type=F32)


def dot_nn(a, b):
    return jnp.dot(a, b, preferred_element_type=F32)


def long_dot(a_ref, b_ref, tile):
    width = a_ref.shape[-1]
    total = dot_nt(a_ref[:, 0:tile], b_ref[:, 0:tile])
    for at in range(tile, width, tile):
        total = total + dot_nt(a_ref[:, at : at + tile], b_ref[:, at : at + tile])
    return total


def split_dot_left(wide, narrow):
    high = wide.astype(BF16)
    low = (wide - high.astype(F32)).astype(BF16)
    return dot_nn(high, narrow) + dot_nn(low, narrow)


def split_dot_right(narrow, wide):
    high = wide.astype(BF16)
    low = (wide - high.astype(F32)).astype(BF16)
    return dot_nn(narrow, high) + dot_nn(narrow, low)


def forward_spans(anchor, n):
    first = 1 - anchor // (n // 2)
    return first, first + (anchor + 1) // n


def backward_span(anchor, step, n):
    section = (anchor - step + n) % n
    return 1 - (section + step) // n


def exchange_kernel(
    n, reps, parts,
    ent, ret, down, up, stash, docs,
    buf, upbuf, gbuf, docbuf, cbuf,
    ent_v, ret_v, down_v, up_v, stash_v, wfull, gsrc, msrc, mbuf, csrc,
    local_sem, send_sem, recv_sem,
):
    s = lax.axis_index("section")
    r = lax.axis_index("dp")
    chips = reps // 2
    chip, core = r // 2, r % 2
    tok, width = ent.shape
    rank = up.shape[1]
    share = width // reps
    wide = buf.shape[-1]
    tile = min(2048, width)

    def sec(shift):
        return (s + shift + n) % n

    def rep(dc, e):
        return ((chip + dc + chips) % chips) * 2 + (core + e) % 2

    def cols(replica):
        return pl.ds(pl.multiple_of(replica * share // wide * wide, 128), wide)

    def piece(replica):
        return pl.ds(pl.multiple_of(replica * share, 128), share)

    inner = pl.ds(pl.multiple_of(r * share % wide, 128), share)
    slots = [(d // 2, d % 2) for d in range(reps)]
    counts = {"copy": 0, "local": 0}
    copies = []
    locals_ = []

    def send(src, dst, section, replica):
        at = counts["copy"]
        counts["copy"] += 1
        copy = pltpu.make_async_remote_copy(
            src_ref=src, dst_ref=dst, send_sem=send_sem.at[at], recv_sem=recv_sem.at[at],
            device_id=(section, replica), device_id_type=pl.DeviceIdType.MESH,
        )
        copy.start()
        copies.append(copy)
        return copy

    def keep(src, dst):
        at = counts["local"]
        counts["local"] += 1
        copy = pltpu.make_async_copy(src, dst, local_sem.at[at])
        copy.start()
        return copy

    load_ent = keep(ent, ent_v)
    load_down = keep(down, down_v)
    load_up = keep(up, up_v)
    load_ret = keep(ret, ret_v)
    load_stash = keep(stash.at[0], stash_v.at[0])
    own_chunk = keep(ent.at[:, cols(r)], buf.at[0, 0])
    own_up = keep(up.at[:, :, cols(r)], upbuf.at[0])
    own_docs = keep(docs, docbuf.at[0])

    barrier = pltpu.get_barrier_semaphore()
    peers = 0
    for shift in (0, 1, 2, -1, -2):
        for dc, e in slots:
            if shift == 0 and dc == 0 and e == 0:
                continue
            pl.semaphore_signal(
                barrier, inc=1, device_id=(sec(shift), rep(dc, e)),
                device_id_type=pl.DeviceIdType.MESH,
            )
            peers += 1
    pl.semaphore_wait(barrier, peers)

    half = tok // parts
    bands = [pl.ds(b * half, half) for b in range(parts)]
    pieces = [("e", 0, b) for b in range(parts)] + [("u", 0, 0), ("u", 1, 0)]
    pieces += [("e", d, b) for d in range(1, reps) for b in range(parts)]
    inside, ahead, across = {}, {}, {}
    arrived = set()
    odd = s % 2
    partner = s + 1 - 2 * odd

    def send_ahead(at):
        kind, d, b = pieces[at]
        if kind == "u":
            src, dst = up.at[d, :, cols(r)], upbuf.at[2, d]
        else:
            dst = buf.at[2, d, bands[b]]
            if d == 0:
                src = ent.at[bands[b], cols(r)]
            else:
                src = buf.at[0, d, bands[b]]
                if d not in arrived:
                    inside[slots[d]].wait_recv()
                    arrived.add(d)
        ahead[at] = send(src, dst, sec(2), r)

    def send_across(at):
        kind, d, b = pieces[at]
        if kind == "u":
            src, dst = upbuf.at[2 * odd, d], upbuf.at[1, d]
        else:
            src, dst = buf.at[2 * odd, d, bands[b]], buf.at[1, d, bands[b]]
        across[kind, d, b] = send(src, dst, partner, r)

    send_ahead(0)
    send_ahead(1)
    prev = sec(-1)
    w1_piece = send(
        down.at[forward_spans(prev, n)[1], :, piece(r)], wfull.at[0, :, piece(r)], prev, r
    )
    for dc, e in slots[1:]:
        target = rep(dc, e)
        inside[dc, e] = send(ent.at[:, cols(target)], buf.at[0, dc * 2 + e], s, target)
    doc_copies = [send(docs, docbuf.at[dc * 2 + e], s, rep(dc, e)) for dc, e in slots[1:]]
    st1 = send(stash.at[1], stash_v.at[1], sec(1), r)
    st2 = send(stash.at[2], stash_v.at[2], sec(2), r)

    def gather_start(which, own_ref):
        mine = wfull.at[which, :, piece(r)]
        out = {0: send(own_ref, mine, s, rep(0, 1))}
        for dc in range(1, chips):
            out[dc] = send(own_ref, mine, s, rep(dc, 0))
        return out

    def gather_pass(which, out):
        passed = []
        for dc in range(1, chips):
            out[dc].wait_recv()
            theirs = wfull.at[which, :, piece(rep(-dc, 0))]
            passed.append(send(theirs, theirs, s, rep(0, 1)))
        return passed

    def gather_end(out, passed):
        out[0].wait_recv()
        for copy in passed:
            copy.wait_recv()

    def gate(q):
        sigma = 1.0 / (1.0 + jnp.exp(-q))
        return sigma * (1.0 + q * (1.0 - sigma))

    held = {}
    g_copies, m_copies, c_copies = [], [], []
    c0, _ = forward_spans(s, n)
    span1, span2 = backward_span(s, 1, n), backward_span(s, 2, n)
    after = sec(1)

    load_ent.wait()
    load_down.wait()
    z0 = long_dot(ent_v, down_v.at[c0], tile)
    g0 = (z0 / (1.0 + jnp.exp(-z0))).astype(BF16)
    gsrc[:, 0:rank] = g0

    def work0():
        own_chunk.wait()
        own_up.wait()
        w1_piece.wait_recv()
        held["w1"] = gather_start(0, wfull.at[0, :, piece(r)])

    def work1():
        load_up.wait()
        load_ret.wait()
        load_stash.wait()
        a0 = long_dot(up_v.at[1], ret_v, tile)
        dz0 = (a0 * gate(stash_v[0])).astype(BF16)
        csrc[0] = dot_nt(dz0, dz0)
        held["dz0"] = dz0

    def work2():
        held["w1p"] = gather_pass(0, held["w1"])

    def work3():
        held["own3"] = keep(upbuf.at[2, span2, :, inner], wfull.at[2, :, piece(r)])
        held["w3"] = gather_start(2, upbuf.at[2, span2, :, inner])
        gather_end(held["w1"], held["w1p"])
        p01 = long_dot(up_v.at[c0], wfull.at[0], tile)
        z1 = long_dot(ent_v, wfull.at[0], tile) + split_dot_right(g0, p01)
        gsrc[:, rank : 2 * rank] = (z1 / (1.0 + jnp.exp(-z1))).astype(BF16)
        for shift in (1, 2):
            for dc, e in slots:
                g_copies.append(
                    send(gsrc, gbuf.at[shift - 1, dc * 2 + e], sec(shift), rep(dc, e))
                )

    def work4():
        held["w3p"] = gather_pass(2, held["w3"])

    def work5():
        across["u", 0, 0].wait_recv()
        across["u", 1, 0].wait_recv()
        held["own2"] = keep(upbuf.at[1, span1, :, inner], wfull.at[1, :, piece(r)])
        held["w2"] = gather_start(1, upbuf.at[1, span1, :, inner])
        late2, late1 = backward_span(after, 2, n), backward_span(after, 1, n)
        first = keep(upbuf.at[1, late2, :, inner], msrc.at[0])
        second = keep(down.at[late1, :, piece(r)], msrc.at[1])
        first.wait()
        second.wait()
        mbuf[reps] = dot_nt(msrc[0], msrc[1])
        for dc, e in slots:
            m_copies.append(send(mbuf.at[reps], mbuf.at[dc * 2 + e], after, rep(dc, e)))

    def work6():
        held["w2p"] = gather_pass(1, held["w2"])
        gather_end(held["w3"], held["w3p"])
        held["own3"].wait()
        n2 = long_dot(wfull.at[2], down_v.at[1], tile)
        held["a2"] = long_dot(wfull.at[2], ret_v, tile) + split_dot_left(n2, held["dz0"])

    def work7():
        gather_end(held["w2"], held["w2p"])
        held["own2"].wait()
        n1 = long_dot(wfull.at[1], down_v.at[1], tile)
        a1 = long_dot(wfull.at[1], ret_v, tile) + split_dot_left(n1, held["dz0"])
        st1.wait_recv()
        dz1 = (a1 * gate(stash_v[1])).astype(BF16)
        csrc[1] = dot_nt(dz1, dz1)
        for copy in m_copies:
            copy.wait_recv()
        n3 = mbuf[0]
        for d in range(1, reps):
            n3 = n3 + mbuf[d]
        a2 = held["a2"] + split_dot_left(n3, dz1)
        st2.wait_recv()
        dz2 = (a2 * gate(stash_v[2])).astype(BF16)
        csrc[2] = dot_nt(dz2, dz2)
        held["own_c"] = keep(csrc.at[0], cbuf.at[0, 0])
        for step in range(3):
            for dc, e in slots:
                if step == 0 and dc == 0 and e == 0:
                    continue
                c_copies.append(
                    send(csrc.at[step], cbuf.at[step, dc * 2 + e], sec(-step), rep(dc, e))
                )

    works = [work0, work1, work2, work3, work4, work5, work6, work7]
    for at in range(len(pieces)):
        ahead[at].wait_recv()
        if at + 2 < len(pieces):
            send_ahead(at + 2)
        if at == 0:
            works[0]()
            send_across(at)
            continue
        send_across(at)
        if at < len(works):
            works[at]()

    own_docs.wait()
    held["own_c"].wait()
    for copy in doc_copies + g_copies + c_copies:
        copy.wait_recv()
    for (kind, _, _), copy in across.items():
        if kind == "e":
            copy.wait_recv()
    for copy in copies:
        copy.wait_send()
    assert counts["copy"] <= send_sem.shape[0] and counts["local"] <= local_sem.shape[0]


def exchange(ent, ret, down, up, stash, docs, n, reps, wide, parts):
    tok, width = ent.shape
    rank = up.shape[1]
    slots = 140 if reps <= 4 else 60 * reps
    anywhere = pl.BlockSpec(memory_space=pltpu.HBM)
    return pl.pallas_call(
        functools.partial(exchange_kernel, n, reps, parts),
        out_shape=(
            jax.ShapeDtypeStruct((3, reps, tok, wide), BF16),
            jax.ShapeDtypeStruct((3, 2, rank, wide), BF16),
            jax.ShapeDtypeStruct((2, reps, tok, 2 * rank), BF16),
            jax.ShapeDtypeStruct((reps,) + docs.shape, jnp.int32),
            jax.ShapeDtypeStruct((3, reps, rank, rank), F32),
        ),
        in_specs=[anywhere] * 6,
        out_specs=(anywhere,) * 5,
        scratch_shapes=[
            pltpu.VMEM((tok, width), BF16),
            pltpu.VMEM((tok, width), BF16),
            pltpu.VMEM((2, rank, width), BF16),
            pltpu.VMEM((2, rank, width), BF16),
            pltpu.VMEM((3, rank, tok), F32),
            pltpu.VMEM((3, rank, width), BF16),
            pltpu.VMEM((tok, 2 * rank), BF16),
            pltpu.VMEM((2, rank, width // reps), BF16),
            pltpu.VMEM((reps + 1, rank, rank), F32),
            pltpu.VMEM((3, rank, rank), F32),
            pltpu.SemaphoreType.DMA((16,)),
            pltpu.SemaphoreType.DMA((slots,)),
            pltpu.SemaphoreType.DMA((slots,)),
        ],
        compiler_params=pltpu.CompilerParams(
            collective_id=0, has_side_effects=True, vmem_limit_bytes=63 * 1024 * 1024
        ),
        name="exchange",
    )(ent, ret, down, up, stash, docs)


def factor_kernel(n, reps, scale, buf, upbuf, gbuf, weight, old, new, rows):
    s = lax.axis_index("section")
    r = lax.axis_index("dp")
    step = pl.program_id(0)
    _, tokens, wide = buf.shape
    rank = upbuf.shape[2]
    height, block = old.shape
    share = height * pl.num_programs(0)

    @pl.when(step == 0)
    def _():
        piece = min(512, wide)
        back1, back2 = (s - 1 + n) % n, (s - 2 + n) % n
        first1, _ = forward_spans(back1, n)
        first2, second2 = forward_spans(back2, n)

        def fill(at, carry):
            here = pl.ds(pl.multiple_of(at * piece, piece), piece)
            rows[0:tokens, here] = (weight[0] * buf[0, :, here].astype(F32)).astype(BF16)
            act = buf[1, :, here].astype(F32) + dot_nn(
                gbuf[0, :, 0:rank], upbuf[1, first1, :, here]
            )
            act = act.astype(BF16).astype(F32)
            rows[tokens : 2 * tokens, here] = (weight[1] * act).astype(BF16)
            act = buf[2, :, here].astype(F32) + dot_nn(
                gbuf[1, :, 0:rank], upbuf[2, first2, :, here]
            )
            act = act.astype(BF16).astype(F32) + dot_nn(
                gbuf[1, :, rank : 2 * rank], upbuf[1, second2, :, here]
            )
            act = act.astype(BF16).astype(F32)
            rows[2 * tokens : 3 * tokens, here] = (weight[2] * act).astype(BF16)
            return carry

        lax.fori_loop(0, wide // piece, fill, 0)

    width = share * reps
    inside = (r * (width // reps)) % wide if width // reps < wide else 0
    left = pl.multiple_of(inside + step * height, 128)
    right = pl.multiple_of(left // block * block, block)
    total = lax.dot_general(
        rows[:, pl.ds(left, height)], rows[:, pl.ds(right, block)], DOWNWARD,
        preferred_element_type=F32,
    )
    new[...] = 0.75 * old[...] + total * scale


def update_factor(buf, upbuf, gbuf, weight, old, n, reps):
    share, block = old.shape
    _, tokens, wide = buf.shape
    height = min(256, share)
    whole = pl.BlockSpec(memory_space=pltpu.VMEM)
    tile = pl.BlockSpec((height, block), lambda i: (i, 0))
    return pl.pallas_call(
        functools.partial(factor_kernel, n, reps, 0.25 / (3 * tokens)),
        out_shape=jax.ShapeDtypeStruct(old.shape, F32),
        grid=(share // height,),
        in_specs=[whole, whole, whole, whole, tile],
        out_specs=tile,
        scratch_shapes=[pltpu.VMEM((3 * tokens, wide), BF16)],
        compiler_params=pltpu.CompilerParams(vmem_limit_bytes=63 * 1024 * 1024),
        name="factor",
    )(buf, upbuf, gbuf, weight, old)


def shards(
    entering, returning, adapter_down, adapter_up, stashed, doc_ids, input_factor, output_factor
):
    s = lax.axis_index("section")
    n = lax.axis_size("section")
    reps = lax.axis_size("dp")
    tok, width = entering.shape[1:]
    block = input_factor.shape[2]
    steps = stashed.shape[1]
    rank = stashed.shape[2]
    tokens = tok * reps
    wide = max(block, width // reps)
    buf, upbuf, gbuf, docbuf, cbuf = exchange(
        entering[0], returning[0], adapter_down[:, 0], adapter_up[:, 0], stashed[0], doc_ids,
        n, reps, wide, 2,
    )
    anchors = (s - jnp.arange(steps, dtype=jnp.int32)) % n
    mine = jnp.take(docbuf, anchors, axis=1).transpose(1, 0, 2).reshape(steps, tokens)
    same = mine[:, :, None] == jnp.arange(2 * reps, dtype=jnp.int32)
    counts = jnp.sum(same.astype(F32), axis=1)
    length = jnp.sum(jnp.where(same, counts[:, None, :], 0.0), axis=2)
    weight = jnp.sqrt(jnp.sqrt(tok / length))[:, :, None]
    factor = update_factor(
        buf.reshape(steps, tokens, wide), upbuf, gbuf.reshape(2, tokens, 2 * rank), weight,
        input_factor[0], n, reps,
    )
    curv = jnp.sum(cbuf, axis=1)
    second = (s + jnp.arange(steps) < n).astype(F32)
    member = jnp.stack([1.0 - second, second])
    held = jnp.sum(member, axis=1)
    total = jnp.sum(member[:, :, None, None] * curv[None], axis=1)
    divisor = (jnp.maximum(held, 1.0) * tokens)[:, None, None]
    updated = 0.75 * output_factor[:, 0] + 0.25 * total / divisor
    outer = jnp.where((held > 0.0)[:, None, None], updated, output_factor[:, 0])
    return factor[None], outer[:, None]


def solution(mesh):
    in_specs = (
        P("section", "dp", None),
        P("section", "dp", None),
        P(None, "section", None, None),
        P(None, "section", None, None),
        P("section", None, None, "dp"),
        P(None, "dp"),
        P("section", "dp", None),
        P(None, "section", None, None),
    )
    out_specs = (P("section", "dp", None), P(None, "section", None, None))
    return jax.shard_map(shards, mesh=mesh, in_specs=in_specs, out_specs=out_specs, check_vma=False)
```

```python
import functools

import jax
import jax.numpy as jnp
from jax import lax
from jax.experimental import pallas as pl
from jax.experimental.pallas import tpu as pltpu
from jax.sharding import PartitionSpec as P

BF16 = jnp.bfloat16
F32 = jnp.float32
ACROSS = (((1,), (1,)), ((), ()))
DOWNWARD = (((0,), (0,)), ((), ()))


def dot_nt(a, b):
    return lax.dot_general(a, b, ACROSS, preferred_element_type=F32)


def dot_nn(a, b):
    return jnp.dot(a, b, preferred_element_type=F32)


def long_dot(a_ref, b_ref, tile):
    width = a_ref.shape[-1]
    total = dot_nt(a_ref[:, 0:tile], b_ref[:, 0:tile])
    for at in range(tile, width, tile):
        total = total + dot_nt(a_ref[:, at : at + tile], b_ref[:, at : at + tile])
    return total


def split_dot_left(wide, narrow):
    high = wide.astype(BF16)
    low = (wide - high.astype(F32)).astype(BF16)
    return dot_nn(high, narrow) + dot_nn(low, narrow)


def split_dot_right(narrow, wide):
    high = wide.astype(BF16)
    low = (wide - high.astype(F32)).astype(BF16)
    return dot_nn(narrow, high) + dot_nn(narrow, low)


def forward_spans(anchor, n):
    first = 1 - anchor // (n // 2)
    return first, first + (anchor + 1) // n


def backward_span(anchor, step, n):
    section = (anchor - step + n) % n
    return 1 - (section + step) // n


def exchange_kernel(
    n, reps, parts,
    ent, ret, down, up, stash, docs,
    buf, upbuf, gbuf, docbuf, cbuf,
    fleft, fright, bleft, bright, stash_v, gsrc, msrc, mbuf, csrc,
    local_sem, send_sem, recv_sem,
):
    s = lax.axis_index("section")
    r = lax.axis_index("dp")
    chips = reps // 2
    chip, core = r // 2, r % 2
    tok, width = ent.shape
    rank = up.shape[1]
    share = width // reps
    wide = buf.shape[-1]
    tile = min(2048, width)

    def sec(shift):
        return (s + shift + n) % n

    def rep(dc, e):
        return ((chip + dc + chips) % chips) * 2 + (core + e) % 2

    def cols(replica):
        return pl.ds(pl.multiple_of(replica * share // wide * wide, 128), wide)

    def piece(replica):
        return pl.ds(pl.multiple_of(replica * share, 128), share)

    inner = pl.ds(pl.multiple_of(r * share % wide, 128), share)
    slots = [(d // 2, d % 2) for d in range(reps)]
    counts = {"copy": 0, "local": 0}
    copies = []
    locals_ = []

    def send(src, dst, section, replica):
        at = counts["copy"]
        counts["copy"] += 1
        copy = pltpu.make_async_remote_copy(
            src_ref=src, dst_ref=dst, send_sem=send_sem.at[at], recv_sem=recv_sem.at[at],
            device_id=(section, replica), device_id_type=pl.DeviceIdType.MESH,
        )
        copy.start()
        copies.append(copy)
        return copy

    def keep(src, dst):
        at = counts["local"]
        counts["local"] += 1
        copy = pltpu.make_async_copy(src, dst, local_sem.at[at])
        copy.start()
        return copy

    c0, _ = forward_spans(s, n)
    forward_loads = [
        keep(ent, fleft.at[pl.ds(0, tok)]),
        keep(up.at[c0], fleft.at[pl.ds(tok, rank)]),
        keep(down.at[c0], fright.at[pl.ds(0, rank)]),
    ]
    backward_loads = [
        keep(ret, bright.at[pl.ds(0, tok)]),
        keep(down.at[1], bright.at[pl.ds(tok, rank)]),
        keep(up.at[1], bleft.at[pl.ds(0, rank)]),
        keep(stash.at[0], stash_v.at[0]),
    ]
    own_chunk = keep(ent.at[:, cols(r)], buf.at[0, 0])
    own_up = keep(up.at[:, :, cols(r)], upbuf.at[0])
    own_docs = keep(docs, docbuf.at[0])

    barrier = pltpu.get_barrier_semaphore()
    peers = 0
    for shift in (0, 1, 2, -1, -2):
        for dc, e in slots:
            if shift == 0 and dc == 0 and e == 0:
                continue
            pl.semaphore_signal(
                barrier, inc=1, device_id=(sec(shift), rep(dc, e)),
                device_id_type=pl.DeviceIdType.MESH,
            )
            peers += 1
    pl.semaphore_wait(barrier, peers)

    half = tok // parts
    bands = [pl.ds(b * half, half) for b in range(parts)]
    pieces = [("e", 0, b) for b in range(parts)] + [("u", 0, 0), ("u", 1, 0)]
    pieces += [("e", d, b) for d in range(1, reps) for b in range(parts)]
    fulls = [
        (fright, pl.ds(rank, rank)), (bleft, pl.ds(rank, rank)), (bleft, pl.ds(2 * rank, rank))
    ]
    inside, ahead, across = {}, {}, {}
    arrived = set()
    window = 3
    odd = s % 2
    partner = s + 1 - 2 * odd

    def send_ahead(at):
        kind, d, b = pieces[at]
        if kind == "u":
            src, dst = up.at[d, :, cols(r)], upbuf.at[2, d]
        else:
            dst = buf.at[2, d, bands[b]]
            if d == 0:
                src = ent.at[bands[b], cols(r)]
            else:
                src = buf.at[0, d, bands[b]]
                if d not in arrived:
                    inside[slots[d]].wait_recv()
                    arrived.add(d)
        ahead[at] = send(src, dst, sec(2), r)

    def send_across(at):
        kind, d, b = pieces[at]
        if kind == "u":
            src, dst = upbuf.at[2 * odd, d], upbuf.at[1, d]
        else:
            src, dst = buf.at[2 * odd, d, bands[b]], buf.at[1, d, bands[b]]
        across[kind, d, b] = send(src, dst, partner, r)

    for at in range(window):
        send_ahead(at)
    prev = sec(-1)
    w1_piece = send(
        down.at[forward_spans(prev, n)[1], :, piece(r)], fright.at[pl.ds(rank, rank), piece(r)], prev, r
    )
    for dc, e in slots[1:]:
        target = rep(dc, e)
        inside[dc, e] = send(ent.at[:, cols(target)], buf.at[0, dc * 2 + e], s, target)
    doc_copies = [send(docs, docbuf.at[dc * 2 + e], s, rep(dc, e)) for dc, e in slots[1:]]
    st1 = send(stash.at[1], stash_v.at[1], sec(1), r)
    st2 = send(stash.at[2], stash_v.at[2], sec(2), r)

    def gather_start(which, own_ref):
        full, rows = fulls[which]
        mine = full.at[rows, piece(r)]
        out = {0: send(own_ref, mine, s, rep(0, 1))}
        for dc in range(1, chips):
            out[dc] = send(own_ref, mine, s, rep(dc, 0))
        return out

    def gather_pass(which, out):
        passed = []
        for dc in range(1, chips):
            out[dc].wait_recv()
            full, rows = fulls[which]
            theirs = full.at[rows, piece(rep(-dc, 0))]
            passed.append(send(theirs, theirs, s, rep(0, 1)))
        return passed

    def gather_end(out, passed):
        out[0].wait_recv()
        for copy in passed:
            copy.wait_recv()

    def gate(q):
        sigma = 1.0 / (1.0 + jnp.exp(-q))
        return sigma * (1.0 + q * (1.0 - sigma))

    held = {}
    g_copies, m_copies, c_copies = [], [], []
    span1, span2 = backward_span(s, 1, n), backward_span(s, 2, n)
    after = sec(1)

    def work0():
        own_chunk.wait()
        own_up.wait()
        w1_piece.wait_recv()
        held["w1"] = gather_start(0, fright.at[pl.ds(rank, rank), piece(r)])

    def work1():
        for load in forward_loads + backward_loads:
            load.wait()

    def work2():
        held["w1p"] = gather_pass(0, held["w1"])

    def work3():
        held["own3"] = keep(upbuf.at[2, span2, :, inner], bleft.at[pl.ds(2 * rank, rank), piece(r)])
        held["w3"] = gather_start(2, upbuf.at[2, span2, :, inner])
    def work4():
        held["w3p"] = gather_pass(2, held["w3"])
        gather_end(held["w1"], held["w1p"])
        both = long_dot(fleft, fright, tile)
        z = both[0:tok]
        g0 = (z / (1.0 + jnp.exp(-z)))[:, 0:rank].astype(BF16)
        later = lax.broadcasted_iota(jnp.int32, z.shape, 1) >= rank
        z = z + jnp.where(later, split_dot_right(g0, both[tok:]), 0.0)
        gsrc[...] = (z / (1.0 + jnp.exp(-z))).astype(BF16)
        for shift in (1, 2):
            for dc, e in slots:
                g_copies.append(
                    send(gsrc, gbuf.at[shift - 1, dc * 2 + e], sec(shift), rep(dc, e))
                )

    def work5():
        across["u", 0, 0].wait_recv()
        across["u", 1, 0].wait_recv()
        held["own2"] = keep(upbuf.at[1, span1, :, inner], bleft.at[pl.ds(rank, rank), piece(r)])
        held["w2"] = gather_start(1, upbuf.at[1, span1, :, inner])
        late2, late1 = backward_span(after, 2, n), backward_span(after, 1, n)
        first = keep(upbuf.at[1, late2, :, inner], msrc.at[0])
        second = keep(down.at[late1, :, piece(r)], msrc.at[1])
        first.wait()
        second.wait()
        mbuf[reps] = dot_nt(msrc[0], msrc[1])
        for dc, e in slots:
            m_copies.append(send(mbuf.at[reps], mbuf.at[dc * 2 + e], after, rep(dc, e)))

    def work6():
        held["w2p"] = gather_pass(1, held["w2"])

    def work7():
        gather_end(held["w3"], held["w3p"])
        gather_end(held["w2"], held["w2p"])
        held["own3"].wait()
        held["own2"].wait()
        both = long_dot(bleft, bright, tile)
        a0, a1, a2 = [both[i * rank : (i + 1) * rank, 0:tok] for i in range(3)]
        _, n1, n2 = [both[i * rank : (i + 1) * rank, tok : tok + rank] for i in range(3)]
        dz0 = (a0 * gate(stash_v[0])).astype(BF16)
        csrc[0] = dot_nt(dz0, dz0)
        a1 = a1 + split_dot_left(n1, dz0)
        st1.wait_recv()
        dz1 = (a1 * gate(stash_v[1])).astype(BF16)
        csrc[1] = dot_nt(dz1, dz1)
        for copy in m_copies:
            copy.wait_recv()
        n3 = mbuf[0]
        for d in range(1, reps):
            n3 = n3 + mbuf[d]
        a2 = a2 + split_dot_left(n2, dz0) + split_dot_left(n3, dz1)
        st2.wait_recv()
        dz2 = (a2 * gate(stash_v[2])).astype(BF16)
        csrc[2] = dot_nt(dz2, dz2)
        held["own_c"] = keep(csrc.at[0], cbuf.at[0, 0])
        for step in range(3):
            for dc, e in slots:
                if step == 0 and dc == 0 and e == 0:
                    continue
                c_copies.append(
                    send(csrc.at[step], cbuf.at[step, dc * 2 + e], sec(-step), rep(dc, e))
                )

    works = [work0, work1, work2, work3, work4, work5, work6, work7]
    for at in range(len(pieces)):
        ahead[at].wait_recv()
        if at + window < len(pieces):
            send_ahead(at + window)
        if at == 0:
            works[0]()
            send_across(at)
            continue
        send_across(at)
        if at < len(works):
            works[at]()

    own_docs.wait()
    held["own_c"].wait()
    for copy in doc_copies + g_copies + c_copies:
        copy.wait_recv()
    for (kind, _, _), copy in across.items():
        if kind == "e":
            copy.wait_recv()
    for copy in copies:
        copy.wait_send()
    assert counts["copy"] <= send_sem.shape[0] and counts["local"] <= local_sem.shape[0]


def exchange(ent, ret, down, up, stash, docs, n, reps, wide, parts):
    tok, width = ent.shape
    rank = up.shape[1]
    slots = 140 if reps <= 4 else 60 * reps
    anywhere = pl.BlockSpec(memory_space=pltpu.HBM)
    return pl.pallas_call(
        functools.partial(exchange_kernel, n, reps, parts),
        out_shape=(
            jax.ShapeDtypeStruct((3, reps, tok, wide), BF16),
            jax.ShapeDtypeStruct((3, 2, rank, wide), BF16),
            jax.ShapeDtypeStruct((2, reps, tok, 2 * rank), BF16),
            jax.ShapeDtypeStruct((reps,) + docs.shape, jnp.int32),
            jax.ShapeDtypeStruct((3, reps, rank, rank), F32),
        ),
        in_specs=[anywhere] * 6,
        out_specs=(anywhere,) * 5,
        scratch_shapes=[
            pltpu.VMEM((tok + rank, width), BF16),
            pltpu.VMEM((2 * rank, width), BF16),
            pltpu.VMEM((3 * rank, width), BF16),
            pltpu.VMEM((tok + rank, width), BF16),
            pltpu.VMEM((3, rank, tok), F32),
            pltpu.VMEM((tok, 2 * rank), BF16),
            pltpu.VMEM((2, rank, width // reps), BF16),
            pltpu.VMEM((reps + 1, rank, rank), F32),
            pltpu.VMEM((3, rank, rank), F32),
            pltpu.SemaphoreType.DMA((16,)),
            pltpu.SemaphoreType.DMA((slots,)),
            pltpu.SemaphoreType.DMA((slots,)),
        ],
        compiler_params=pltpu.CompilerParams(
            collective_id=0, has_side_effects=True, vmem_limit_bytes=63 * 1024 * 1024
        ),
        name="exchange",
    )(ent, ret, down, up, stash, docs)


def factor_kernel(n, reps, scale, buf, upbuf, gbuf, weight, old, new, rows):
    s = lax.axis_index("section")
    r = lax.axis_index("dp")
    step = pl.program_id(0)
    _, tokens, wide = buf.shape
    rank = upbuf.shape[2]
    height, block = old.shape
    share = height * pl.num_programs(0)

    @pl.when(step == 0)
    def _():
        piece = min(512, wide)
        back1, back2 = (s - 1 + n) % n, (s - 2 + n) % n
        first1, _ = forward_spans(back1, n)
        first2, second2 = forward_spans(back2, n)

        def fill(at, carry):
            here = pl.ds(pl.multiple_of(at * piece, piece), piece)
            rows[0:tokens, here] = (weight[0] * buf[0, :, here].astype(F32)).astype(BF16)
            act = buf[1, :, here].astype(F32) + dot_nn(
                gbuf[0, :, 0:rank], upbuf[1, first1, :, here]
            )
            act = act.astype(BF16).astype(F32)
            rows[tokens : 2 * tokens, here] = (weight[1] * act).astype(BF16)
            act = buf[2, :, here].astype(F32) + dot_nn(
                gbuf[1, :, 0:rank], upbuf[2, first2, :, here]
            )
            act = act.astype(BF16).astype(F32) + dot_nn(
                gbuf[1, :, rank : 2 * rank], upbuf[1, second2, :, here]
            )
            act = act.astype(BF16).astype(F32)
            rows[2 * tokens : 3 * tokens, here] = (weight[2] * act).astype(BF16)
            return carry

        lax.fori_loop(0, wide // piece, fill, 0)

    width = share * reps
    inside = (r * (width // reps)) % wide if width // reps < wide else 0
    left = pl.multiple_of(inside + step * height, 128)
    right = pl.multiple_of(left // block * block, block)
    total = lax.dot_general(
        rows[:, pl.ds(left, height)], rows[:, pl.ds(right, block)], DOWNWARD,
        preferred_element_type=F32,
    )
    new[...] = 0.75 * old[...] + total * scale


def update_factor(buf, upbuf, gbuf, weight, old, n, reps):
    share, block = old.shape
    _, tokens, wide = buf.shape
    height = min(256, share)
    whole = pl.BlockSpec(memory_space=pltpu.VMEM)
    tile = pl.BlockSpec((height, block), lambda i: (i, 0))
    return pl.pallas_call(
        functools.partial(factor_kernel, n, reps, 0.25 / (3 * tokens)),
        out_shape=jax.ShapeDtypeStruct(old.shape, F32),
        grid=(share // height,),
        in_specs=[whole, whole, whole, whole, tile],
        out_specs=tile,
        scratch_shapes=[pltpu.VMEM((3 * tokens, wide), BF16)],
        compiler_params=pltpu.CompilerParams(vmem_limit_bytes=63 * 1024 * 1024),
        name="factor",
    )(buf, upbuf, gbuf, weight, old)


def shards(
    entering, returning, adapter_down, adapter_up, stashed, doc_ids, input_factor, output_factor
):
    s = lax.axis_index("section")
    n = lax.axis_size("section")
    reps = lax.axis_size("dp")
    tok, width = entering.shape[1:]
    block = input_factor.shape[2]
    steps = stashed.shape[1]
    rank = stashed.shape[2]
    tokens = tok * reps
    wide = max(block, width // reps)
    buf, upbuf, gbuf, docbuf, cbuf = exchange(
        entering[0], returning[0], adapter_down[:, 0], adapter_up[:, 0], stashed[0], doc_ids,
        n, reps, wide, 2,
    )
    anchors = (s - jnp.arange(steps, dtype=jnp.int32)) % n
    mine = jnp.take(docbuf, anchors, axis=1).transpose(1, 0, 2).reshape(steps, tokens)
    same = mine[:, :, None] == jnp.arange(2 * reps, dtype=jnp.int32)
    counts = jnp.sum(same.astype(F32), axis=1)
    length = jnp.sum(jnp.where(same, counts[:, None, :], 0.0), axis=2)
    weight = jnp.sqrt(jnp.sqrt(tok / length))[:, :, None]
    factor = update_factor(
        buf.reshape(steps, tokens, wide), upbuf, gbuf.reshape(2, tokens, 2 * rank), weight,
        input_factor[0], n, reps,
    )
    curv = jnp.sum(cbuf, axis=1)
    second = (s + jnp.arange(steps) < n).astype(F32)
    member = jnp.stack([1.0 - second, second])
    held = jnp.sum(member, axis=1)
    total = jnp.sum(member[:, :, None, None] * curv[None], axis=1)
    divisor = (jnp.maximum(held, 1.0) * tokens)[:, None, None]
    updated = 0.75 * output_factor[:, 0] + 0.25 * total / divisor
    outer = jnp.where((held > 0.0)[:, None, None], updated, output_factor[:, 0])
    return factor[None], outer[:, None]


def solution(mesh):
    in_specs = (
        P("section", "dp", None),
        P("section", "dp", None),
        P(None, "section", None, None),
        P(None, "section", None, None),
        P("section", None, None, "dp"),
        P(None, "dp"),
        P("section", "dp", None),
        P(None, "section", None, None),
    )
    out_specs = (P("section", "dp", None), P(None, "section", None, None))
    return jax.shard_map(shards, mesh=mesh, in_specs=in_specs, out_specs=out_specs, check_vma=False)
```

```python
import functools

import jax
import jax.numpy as jnp
from jax import lax
from jax.experimental import pallas as pl
from jax.experimental.pallas import tpu as pltpu
from jax.sharding import PartitionSpec as P

BF16 = jnp.bfloat16
F32 = jnp.float32
ACROSS = (((1,), (1,)), ((), ()))
DOWNWARD = (((0,), (0,)), ((), ()))


def dot_nt(a, b):
    return lax.dot_general(a, b, ACROSS, preferred_element_type=F32)


def dot_nn(a, b):
    return jnp.dot(a, b, preferred_element_type=F32)


def long_dot(a_ref, b_ref, tile):
    width = a_ref.shape[-1]
    total = dot_nt(a_ref[:, 0:tile], b_ref[:, 0:tile])
    for at in range(tile, width, tile):
        total = total + dot_nt(a_ref[:, at : at + tile], b_ref[:, at : at + tile])
    return total


def split_dot_left(wide, narrow):
    high = wide.astype(BF16)
    low = (wide - high.astype(F32)).astype(BF16)
    return dot_nn(high, narrow) + dot_nn(low, narrow)


def split_dot_right(narrow, wide):
    high = wide.astype(BF16)
    low = (wide - high.astype(F32)).astype(BF16)
    return dot_nn(narrow, high) + dot_nn(narrow, low)


def forward_spans(anchor, n):
    first = 1 - anchor // (n // 2)
    return first, first + (anchor + 1) // n


def backward_span(anchor, step, n):
    section = (anchor - step + n) % n
    return 1 - (section + step) // n


def exchange_kernel(
    n, reps, parts,
    ent, ret, down, up, stash, docs, old,
    base, tail, cbuf,
    buf, upbuf, gbuf, docbuf, weight, rows, total,
    fleft, fright, bleft, bright, stash_v, gsrc, msrc, mbuf, csrc,
    local_sem, send_sem, recv_sem,
):
    s = lax.axis_index("section")
    r = lax.axis_index("dp")
    chips = reps // 2
    chip, core = r // 2, r % 2
    tok, width = ent.shape
    rank = up.shape[1]
    share = width // reps
    wide = buf.shape[-1]
    tile = min(2048, width)

    def sec(shift):
        return (s + shift + n) % n

    def rep(dc, e):
        return ((chip + dc + chips) % chips) * 2 + (core + e) % 2

    def cols(replica):
        return pl.ds(pl.multiple_of(replica * share // wide * wide, 128), wide)

    def piece(replica):
        return pl.ds(pl.multiple_of(replica * share, 128), share)

    inner = pl.ds(pl.multiple_of(r * share % wide, 128), share)
    slots = [(d // 2, d % 2) for d in range(reps)]
    counts = {"copy": 0, "local": 0}
    copies = []
    locals_ = []

    def send(src, dst, section, replica):
        at = counts["copy"]
        counts["copy"] += 1
        copy = pltpu.make_async_remote_copy(
            src_ref=src, dst_ref=dst, send_sem=send_sem.at[at], recv_sem=recv_sem.at[at],
            device_id=(section, replica), device_id_type=pl.DeviceIdType.MESH,
        )
        copy.start()
        copies.append(copy)
        return copy

    def keep(src, dst):
        at = counts["local"]
        counts["local"] += 1
        copy = pltpu.make_async_copy(src, dst, local_sem.at[at])
        copy.start()
        return copy

    c0, _ = forward_spans(s, n)
    forward_loads = [
        keep(ent, fleft.at[pl.ds(0, tok)]),
        keep(up.at[c0], fleft.at[pl.ds(tok, rank)]),
        keep(down.at[c0], fright.at[pl.ds(0, rank)]),
    ]
    backward_loads = [
        keep(ret, bright.at[pl.ds(0, tok)]),
        keep(down.at[1], bright.at[pl.ds(tok, rank)]),
        keep(up.at[1], bleft.at[pl.ds(0, rank)]),
        keep(stash.at[0], stash_v.at[0]),
    ]
    own_chunk = keep(ent.at[:, cols(r)], buf.at[0, 0])
    own_up = keep(up.at[:, :, cols(r)], upbuf.at[0])
    own_docs = keep(docs, docbuf.at[0])
    load_old = keep(old, total)

    barrier = pltpu.get_barrier_semaphore()
    peers = 0
    for shift in (0, 1, 2, -1, -2):
        for dc, e in slots:
            if shift == 0 and dc == 0 and e == 0:
                continue
            pl.semaphore_signal(
                barrier, inc=1, device_id=(sec(shift), rep(dc, e)),
                device_id_type=pl.DeviceIdType.MESH,
            )
            peers += 1
    pl.semaphore_wait(barrier, peers)

    half = tok // parts
    bands = [pl.ds(b * half, half) for b in range(parts)]
    pieces = [("e", 0, b) for b in range(parts)] + [("u", 0, 0), ("u", 1, 0)]
    pieces += [("e", d, b) for d in range(1, reps) for b in range(parts)]
    fulls = [
        (fright, pl.ds(rank, rank)), (bleft, pl.ds(rank, rank)), (bleft, pl.ds(2 * rank, rank))
    ]
    inside, ahead, across = {}, {}, {}
    arrived = set()
    odd = s % 2
    partner = s + 1 - 2 * odd

    def send_ahead(at):
        kind, d, b = pieces[at]
        if kind == "u":
            src, dst = up.at[d, :, cols(r)], upbuf.at[2, d]
        else:
            dst = buf.at[2, d, bands[b]]
            if d == 0:
                src = ent.at[bands[b], cols(r)]
            else:
                src = buf.at[0, d, bands[b]]
                if d not in arrived:
                    inside[slots[d]].wait_recv()
                    arrived.add(d)
        ahead[at] = send(src, dst, sec(2), r)

    def send_across(at):
        kind, d, b = pieces[at]
        if kind == "u":
            src, dst = upbuf.at[2 * odd, d], upbuf.at[1, d]
        else:
            src, dst = buf.at[2 * odd, d, bands[b]], buf.at[1, d, bands[b]]
        across[kind, d, b] = send(src, dst, partner, r)

    for at in range(2 * parts):
        send_ahead(at)
    prev = sec(-1)
    w1_piece = send(
        down.at[forward_spans(prev, n)[1], :, piece(r)], fright.at[pl.ds(rank, rank), piece(r)], prev, r
    )
    for dc, e in slots[1:]:
        target = rep(dc, e)
        inside[dc, e] = send(ent.at[:, cols(target)], buf.at[0, dc * 2 + e], s, target)
    doc_copies = [send(docs, docbuf.at[dc * 2 + e], s, rep(dc, e)) for dc, e in slots[1:]]
    st1 = send(stash.at[1], stash_v.at[1], sec(1), r)
    st2 = send(stash.at[2], stash_v.at[2], sec(2), r)

    def gather_start(which, own_ref):
        full, rows = fulls[which]
        mine = full.at[rows, piece(r)]
        out = {0: send(own_ref, mine, s, rep(0, 1))}
        for dc in range(1, chips):
            out[dc] = send(own_ref, mine, s, rep(dc, 0))
        return out

    def gather_pass(which, out):
        passed = []
        for dc in range(1, chips):
            out[dc].wait_recv()
            full, rows = fulls[which]
            theirs = full.at[rows, piece(rep(-dc, 0))]
            passed.append(send(theirs, theirs, s, rep(0, 1)))
        return passed

    def gather_end(out, passed):
        out[0].wait_recv()
        for copy in passed:
            copy.wait_recv()

    def gate(q):
        sigma = 1.0 / (1.0 + jnp.exp(-q))
        return sigma * (1.0 + q * (1.0 - sigma))

    block = total.shape[1]
    height = min(256, share)
    scale = 0.25 / (3 * tok * reps)

    def weigh():
        own_docs.wait()
        for copy in doc_copies:
            copy.wait_recv()
        ids = docbuf[...]
        length = jnp.zeros(ids.shape, F32)
        for doc in range(2 * reps):
            same = jnp.where(ids == doc, 1.0, 0.0)
            count = jnp.sum(jnp.sum(same, axis=0), axis=1, keepdims=True)
            length = length + same * count[None]
        weight[...] = jnp.sqrt(jnp.sqrt(tok / length))

    def column(slot, d):
        own = weight[d]
        mine = lax.broadcasted_iota(jnp.int32, own.shape, 0) == sec(-slot)
        line = jnp.sum(jnp.where(mine, own, 0.0), axis=0, keepdims=True)
        square = jnp.broadcast_to(line, (tok, tok))
        across_, along = [lax.broadcasted_iota(jnp.int32, (tok, tok), i) for i in (0, 1)]
        return jnp.sum(jnp.where(across_ == along, square, 0.0), axis=1, keepdims=True)

    back1, back2 = sec(-1), sec(-2)
    first1, _ = forward_spans(back1, n)
    first2, second2 = forward_spans(back2, n)
    strip = min(512, wide)

    def form(slot, d, place):
        scaled = column(slot, d)
        here = pl.ds(place * tok, tok)

        def fill(at, carry):
            on = pl.ds(pl.multiple_of(at * strip, strip), strip)
            act = buf[slot, d, :, on].astype(F32)
            if slot == 1:
                act = act + dot_nn(gbuf[0, d, :, 0:rank], upbuf[1, first1, :, on])
                act = act.astype(BF16).astype(F32)
            if slot == 2:
                act = act + dot_nn(gbuf[1, d, :, 0:rank], upbuf[2, first2, :, on])
                act = act.astype(BF16).astype(F32)
                act = act + dot_nn(gbuf[1, d, :, rank : 2 * rank], upbuf[1, second2, :, on])
                act = act.astype(BF16).astype(F32)
            rows[here, on] = (scaled * act).astype(BF16)
            return carry

        lax.fori_loop(0, wide // strip, fill, 0)

    def products(decay):
        offset = r * share % wide

        def one(at, carry):
            left = pl.multiple_of(offset + at * height, 128)
            right = pl.multiple_of(left // block * block, block)
            here = pl.ds(pl.multiple_of(at * height, height), height)
            gram = lax.dot_general(
                rows[:, pl.ds(left, height)], rows[:, pl.ds(right, block)], DOWNWARD,
                preferred_element_type=F32,
            )
            total[here] = decay * total[here] + gram * scale
            return carry

        lax.fori_loop(0, share // height, one, 0)

    held = {}
    g_copies, m_copies, c_copies = [], [], []
    span1, span2 = backward_span(s, 1, n), backward_span(s, 2, n)
    after = sec(1)

    def work0():
        own_chunk.wait()
        own_up.wait()
        w1_piece.wait_recv()
        held["w1"] = gather_start(0, fright.at[pl.ds(rank, rank), piece(r)])

    def work1():
        for load in forward_loads + backward_loads:
            load.wait()

    def work2():
        held["w1p"] = gather_pass(0, held["w1"])

    def work3():
        held["own3"] = keep(upbuf.at[2, span2, :, inner], bleft.at[pl.ds(2 * rank, rank), piece(r)])
        held["w3"] = gather_start(2, upbuf.at[2, span2, :, inner])
    def work4():
        held["w3p"] = gather_pass(2, held["w3"])
        gather_end(held["w1"], held["w1p"])
        both = long_dot(fleft, fright, tile)
        z = both[0:tok]
        g0 = (z / (1.0 + jnp.exp(-z)))[:, 0:rank].astype(BF16)
        later = lax.broadcasted_iota(jnp.int32, z.shape, 1) >= rank
        z = z + jnp.where(later, split_dot_right(g0, both[tok:]), 0.0)
        gsrc[...] = (z / (1.0 + jnp.exp(-z))).astype(BF16)
        for shift in (1, 2):
            for dc, e in slots:
                g_copies.append(
                    send(gsrc, gbuf.at[shift - 1, dc * 2 + e], sec(shift), rep(dc, e))
                )

    def work5():
        across["u", 0, 0].wait_recv()
        across["u", 1, 0].wait_recv()
        held["own2"] = keep(upbuf.at[1, span1, :, inner], bleft.at[pl.ds(rank, rank), piece(r)])
        held["w2"] = gather_start(1, upbuf.at[1, span1, :, inner])
        late2, late1 = backward_span(after, 2, n), backward_span(after, 1, n)
        first = keep(upbuf.at[1, late2, :, inner], msrc.at[0])
        second = keep(down.at[late1, :, piece(r)], msrc.at[1])
        first.wait()
        second.wait()
        mbuf[reps] = dot_nt(msrc[0], msrc[1])
        for dc, e in slots:
            m_copies.append(send(mbuf.at[reps], mbuf.at[dc * 2 + e], after, rep(dc, e)))

    def work6():
        held["w2p"] = gather_pass(1, held["w2"])

    def work7():
        gather_end(held["w3"], held["w3p"])
        gather_end(held["w2"], held["w2p"])
        held["own3"].wait()
        held["own2"].wait()
        both = long_dot(bleft, bright, tile)
        a0, a1, a2 = [both[i * rank : (i + 1) * rank, 0:tok] for i in range(3)]
        _, n1, n2 = [both[i * rank : (i + 1) * rank, tok : tok + rank] for i in range(3)]
        dz0 = (a0 * gate(stash_v[0])).astype(BF16)
        csrc[0] = dot_nt(dz0, dz0)
        a1 = a1 + split_dot_left(n1, dz0)
        st1.wait_recv()
        dz1 = (a1 * gate(stash_v[1])).astype(BF16)
        csrc[1] = dot_nt(dz1, dz1)
        for copy in m_copies:
            copy.wait_recv()
        n3 = mbuf[0]
        for d in range(1, reps):
            n3 = n3 + mbuf[d]
        a2 = a2 + split_dot_left(n2, dz0) + split_dot_left(n3, dz1)
        st2.wait_recv()
        dz2 = (a2 * gate(stash_v[2])).astype(BF16)
        csrc[2] = dot_nt(dz2, dz2)
        held["own_c"] = keep(csrc.at[0], cbuf.at[0, 0])
        for step in range(3):
            for dc, e in slots:
                if step == 0 and dc == 0 and e == 0:
                    continue
                c_copies.append(
                    send(csrc.at[step], cbuf.at[step, dc * 2 + e], sec(-step), rep(dc, e))
                )

    works = [work0, work1, work2, work3, work4, work5, work6, work7]
    started = set(range(2 * parts))

    def arrive(d):
        for at, (kind, of, _) in enumerate(pieces):
            if kind == "e" and of == d and at not in started:
                started.add(at)
                send_ahead(at)

    def own_products(start):
        for d in range(start, start + 4):
            form(0, d, d - start)
        products(0.75 if start == 0 else 1.0)

    def relayed(start):
        for place, (slot, d) in enumerate([(1, start), (2, start), (1, start + 1), (2, start + 1)]):
            form(slot, d, place)

    waited = set()

    def wait_across(d):
        for b in range(parts):
            if (d, b) not in waited:
                waited.add((d, b))
                across["e", d, b].wait_recv()

    for at in range(len(pieces)):
        if at == 1:
            arrive(1)
        if at == 3:
            for d in range(2, reps):
                arrive(d)
        ahead[at].wait_recv()
        if at == 0:
            works[0]()
        send_across(at)
        if 0 < at < len(works):
            works[at]()
        if at == 4:
            weigh()
            load_old.wait()
            own_products(0)
    for start in range(4, reps, 4):
        own_products(start)
    for copy in g_copies:
        copy.wait_recv()
    for start in range(0, reps, 2):
        wait_across(start)
        wait_across(start + 1)
        relayed(start)
        if start + 2 < reps:
            products(1.0)
    write_base = keep(total, base)
    write_tail = keep(rows, tail)
    held["own_c"].wait()
    for copy in c_copies:
        copy.wait_recv()
    write_base.wait()
    write_tail.wait()
    for copy in copies:
        copy.wait_send()
    assert counts["copy"] <= send_sem.shape[0] and counts["local"] <= local_sem.shape[0]


def exchange(ent, ret, down, up, stash, docs, old, n, reps, wide, parts):
    tok, width = ent.shape
    rank = up.shape[1]
    slots = 140 if reps <= 4 else 60 * reps
    anywhere = pl.BlockSpec(memory_space=pltpu.HBM)
    return pl.pallas_call(
        functools.partial(exchange_kernel, n, reps, parts),
        out_shape=(
            jax.ShapeDtypeStruct(old.shape, F32),
            jax.ShapeDtypeStruct((4 * tok, wide), BF16),
            jax.ShapeDtypeStruct((3, reps, rank, rank), F32),
        ),
        in_specs=[anywhere] * 7,
        out_specs=(anywhere,) * 3,
        scratch_shapes=[
            pltpu.VMEM((3, reps, tok, wide), BF16),
            pltpu.VMEM((3, 2, rank, wide), BF16),
            pltpu.VMEM((2, reps, tok, 2 * rank), BF16),
            pltpu.VMEM((reps,) + docs.shape, jnp.int32),
            pltpu.VMEM((reps,) + docs.shape, F32),
            pltpu.VMEM((4 * tok, wide), BF16),
            pltpu.VMEM(old.shape, F32),
            pltpu.VMEM((tok + rank, width), BF16),
            pltpu.VMEM((2 * rank, width), BF16),
            pltpu.VMEM((3 * rank, width), BF16),
            pltpu.VMEM((tok + rank, width), BF16),
            pltpu.VMEM((3, rank, tok), F32),
            pltpu.VMEM((tok, 2 * rank), BF16),
            pltpu.VMEM((2, rank, width // reps), BF16),
            pltpu.VMEM((reps + 1, rank, rank), F32),
            pltpu.VMEM((3, rank, rank), F32),
            pltpu.SemaphoreType.DMA((24,)),
            pltpu.SemaphoreType.DMA((slots,)),
            pltpu.SemaphoreType.DMA((slots,)),
        ],
        compiler_params=pltpu.CompilerParams(
            collective_id=0, has_side_effects=True, vmem_limit_bytes=63 * 1024 * 1024
        ),
        name="exchange",
    )(ent, ret, down, up, stash, docs, old)


def factor_kernel(n, reps, base_rows, scale, tokens, rows, cbuf, outer, base, new, outer_new):
    s = lax.axis_index("section")
    r = lax.axis_index("dp")
    step = pl.program_id(0)
    wide = rows.shape[1]
    height, block = base.shape
    share = base_rows
    inside = (r * share) % wide if share < wide else 0
    left = pl.multiple_of(inside + step * height, 128)
    right = pl.multiple_of(left // block * block, block)
    total = lax.dot_general(
        rows[:, pl.ds(left, height)], rows[:, pl.ds(right, block)], DOWNWARD,
        preferred_element_type=F32,
    )
    new[...] = base[...] + total * scale

    @pl.when(step == 0)
    def _():
        for span in range(2):
            sums = jnp.zeros(outer.shape[1:], F32)
            held = jnp.int32(0)
            for at in range(3):
                second = 1 - (s + at) // n
                member = second if span == 1 else 1 - second
                curv = cbuf[at, 0]
                for d in range(1, reps):
                    curv = curv + cbuf[at, d]
                sums = sums + jnp.where(member == 1, curv, 0.0)
                held = held + member
            divisor = jnp.maximum(held, 1).astype(F32) * tokens
            updated = 0.75 * outer[span] + 0.25 * sums / divisor
            outer_new[span] = jnp.where(held > 0, updated, outer[span])


def update_factor(rows, cbuf, outer, base, n, reps, tokens):
    share, block = base.shape
    height = min(256, share)
    whole = pl.BlockSpec(memory_space=pltpu.VMEM)
    tile = pl.BlockSpec((height, block), lambda i: (i, 0))
    return pl.pallas_call(
        functools.partial(factor_kernel, n, reps, share, 0.25 / (3 * tokens), tokens),
        out_shape=(
            jax.ShapeDtypeStruct(base.shape, F32), jax.ShapeDtypeStruct(outer.shape, F32)
        ),
        grid=(share // height,),
        in_specs=[whole, whole, whole, tile],
        out_specs=(tile, pl.BlockSpec(outer.shape, lambda i: (0, 0, 0))),
        compiler_params=pltpu.CompilerParams(vmem_limit_bytes=63 * 1024 * 1024),
        name="factor",
    )(rows, cbuf, outer, base)


def shards(
    entering, returning, adapter_down, adapter_up, stashed, doc_ids, input_factor, output_factor
):
    n = lax.axis_size("section")
    reps = lax.axis_size("dp")
    tok, width = entering.shape[1:]
    block = input_factor.shape[2]
    wide = max(block, width // reps)
    base, tail, cbuf = exchange(
        entering[0], returning[0], adapter_down[:, 0], adapter_up[:, 0], stashed[0], doc_ids,
        input_factor[0], n, reps, wide, 2,
    )
    factor, outer = update_factor(tail, cbuf, output_factor[:, 0], base, n, reps, tok * reps)
    return factor[None], outer[:, None]


def solution(mesh):
    in_specs = (
        P("section", "dp", None),
        P("section", "dp", None),
        P(None, "section", None, None),
        P(None, "section", None, None),
        P("section", None, None, "dp"),
        P(None, "dp"),
        P("section", "dp", None),
        P(None, "section", None, None),
    )
    out_specs = (P("section", "dp", None), P(None, "section", None, None))
    return jax.shard_map(shards, mesh=mesh, in_specs=in_specs, out_specs=out_specs, check_vma=False)
```

```python
import functools

import jax
import jax.numpy as jnp
from jax import lax
from jax.experimental import pallas as pl
from jax.experimental.pallas import tpu as pltpu
from jax.sharding import PartitionSpec as P

BF16 = jnp.bfloat16
F32 = jnp.float32
ACROSS = (((1,), (1,)), ((), ()))
DOWNWARD = (((0,), (0,)), ((), ()))


def dot_nt(a, b):
    return lax.dot_general(a, b, ACROSS, preferred_element_type=F32)


def dot_nn(a, b):
    return jnp.dot(a, b, preferred_element_type=F32)


def long_dot(a_ref, b_ref, tile):
    width = a_ref.shape[-1]
    total = dot_nt(a_ref[:, 0:tile], b_ref[:, 0:tile])
    for at in range(tile, width, tile):
        total = total + dot_nt(a_ref[:, at : at + tile], b_ref[:, at : at + tile])
    return total


def split_dot_left(wide, narrow):
    high = wide.astype(BF16)
    low = (wide - high.astype(F32)).astype(BF16)
    return dot_nn(high, narrow) + dot_nn(low, narrow)


def split_dot_right(narrow, wide):
    high = wide.astype(BF16)
    low = (wide - high.astype(F32)).astype(BF16)
    return dot_nn(narrow, high) + dot_nn(narrow, low)


def forward_spans(anchor, n):
    first = 1 - anchor // (n // 2)
    return first, first + (anchor + 1) // n


def backward_span(anchor, step, n):
    section = (anchor - step + n) % n
    return 1 - (section + step) // n


def exchange_kernel(
    n, reps, parts,
    ent, ret, down, up, stash, docs, old,
    base, tail, cbuf,
    buf, upbuf, gbuf, docbuf, weight, rows, total,
    fleft, fright, bleft, bright, stash_v, gsrc, msrc, mbuf, csrc,
    local_sem, send_sem, recv_sem,
):
    s = lax.axis_index("section")
    r = lax.axis_index("dp")
    chips = reps // 2
    chip, core = r // 2, r % 2
    tok, width = ent.shape
    rank = up.shape[1]
    share = width // reps
    wide = buf.shape[-1]
    tile = min(2048, width)

    def sec(shift):
        return (s + shift + n) % n

    def rep(dc, e):
        return ((chip + dc + chips) % chips) * 2 + (core + e) % 2

    def cols(replica):
        return pl.ds(pl.multiple_of(replica * share // wide * wide, 128), wide)

    def piece(replica):
        return pl.ds(pl.multiple_of(replica * share, 128), share)

    inner = pl.ds(pl.multiple_of(r * share % wide, 128), share)
    slots = [(d // 2, d % 2) for d in range(reps)]
    counts = {"copy": 0, "local": 0}
    copies = []
    locals_ = []

    def send(src, dst, section, replica):
        at = counts["copy"]
        counts["copy"] += 1
        copy = pltpu.make_async_remote_copy(
            src_ref=src, dst_ref=dst, send_sem=send_sem.at[at], recv_sem=recv_sem.at[at],
            device_id=(section, replica), device_id_type=pl.DeviceIdType.MESH,
        )
        copy.start()
        copies.append(copy)
        return copy

    def keep(src, dst):
        at = counts["local"]
        counts["local"] += 1
        copy = pltpu.make_async_copy(src, dst, local_sem.at[at])
        copy.start()
        return copy

    c0, _ = forward_spans(s, n)
    forward_loads = [
        keep(ent, fleft.at[pl.ds(0, tok)]),
        keep(up.at[c0], fleft.at[pl.ds(tok, rank)]),
        keep(down.at[c0], fright.at[pl.ds(0, rank)]),
    ]
    backward_loads = [
        keep(ret, bright.at[pl.ds(0, tok)]),
        keep(down.at[1], bright.at[pl.ds(tok, rank)]),
        keep(up.at[1], bleft.at[pl.ds(0, rank)]),
        keep(stash.at[0], stash_v.at[0]),
    ]
    own_chunk = keep(ent.at[:, cols(r)], buf.at[0, 0])
    own_up = keep(up.at[:, :, cols(r)], upbuf.at[0])
    own_docs = keep(docs, docbuf.at[0])
    load_old = keep(old, total)

    barrier = pltpu.get_barrier_semaphore()
    peers = 0
    for shift in (0, 1, 2, -1, -2):
        for dc, e in slots:
            if shift == 0 and dc == 0 and e == 0:
                continue
            pl.semaphore_signal(
                barrier, inc=1, device_id=(sec(shift), rep(dc, e)),
                device_id_type=pl.DeviceIdType.MESH,
            )
            peers += 1
    pl.semaphore_wait(barrier, peers)

    half = tok // parts
    bands = [pl.ds(b * half, half) for b in range(parts)]
    pieces = [("e", 0, b) for b in range(parts)] + [("u", 0, 0), ("u", 1, 0)]
    pieces += [("e", d, b) for d in range(1, reps) for b in range(parts)]
    fulls = [
        (fright, pl.ds(rank, rank)), (bleft, pl.ds(rank, rank)), (bleft, pl.ds(2 * rank, rank))
    ]
    inside, ahead, across = {}, {}, {}
    arrived = set()
    odd = s % 2
    partner = s + 1 - 2 * odd

    def send_ahead(at):
        kind, d, b = pieces[at]
        if kind == "u":
            src, dst = up.at[d, :, cols(r)], upbuf.at[2, d]
        else:
            dst = buf.at[2, d, bands[b]]
            if d == 0:
                src = ent.at[bands[b], cols(r)]
            else:
                src = buf.at[0, d, bands[b]]
                if d not in arrived:
                    inside[slots[d]].wait_recv()
                    arrived.add(d)
        ahead[at] = send(src, dst, sec(2), r)

    def send_across(at):
        kind, d, b = pieces[at]
        if kind == "u":
            src, dst = upbuf.at[2 * odd, d], upbuf.at[1, d]
        else:
            src, dst = buf.at[2 * odd, d, bands[b]], buf.at[1, d, bands[b]]
        across[kind, d, b] = send(src, dst, partner, r)

    for at in range(2 * parts):
        send_ahead(at)
    prev = sec(-1)
    w1_piece = send(
        down.at[forward_spans(prev, n)[1], :, piece(r)], fright.at[pl.ds(rank, rank), piece(r)], prev, r
    )
    for dc, e in slots[1:]:
        target = rep(dc, e)
        inside[dc, e] = send(ent.at[:, cols(target)], buf.at[0, dc * 2 + e], s, target)
    doc_copies = [send(docs, docbuf.at[dc * 2 + e], s, rep(dc, e)) for dc, e in slots[1:]]
    st1 = send(stash.at[1], stash_v.at[1], sec(1), r)
    st2 = send(stash.at[2], stash_v.at[2], sec(2), r)

    def gather_start(which, own_ref):
        full, rows = fulls[which]
        mine = full.at[rows, piece(r)]
        out = {0: send(own_ref, mine, s, rep(0, 1))}
        for dc in range(1, chips):
            out[dc] = send(own_ref, mine, s, rep(dc, 0))
        return out

    def gather_pass(which, out):
        passed = []
        for dc in range(1, chips):
            out[dc].wait_recv()
            full, rows = fulls[which]
            theirs = full.at[rows, piece(rep(-dc, 0))]
            passed.append(send(theirs, theirs, s, rep(0, 1)))
        return passed

    def gather_end(out, passed):
        out[0].wait_recv()
        for copy in passed:
            copy.wait_recv()

    def gate(q):
        sigma = 1.0 / (1.0 + jnp.exp(-q))
        return sigma * (1.0 + q * (1.0 - sigma))

    block = total.shape[1]
    height = min(256, share)
    scale = 0.25 / (3 * tok * reps)

    def weigh():
        own_docs.wait()
        for copy in doc_copies:
            copy.wait_recv()
        ids = docbuf[...]
        length = jnp.zeros(ids.shape, F32)
        for doc in range(2 * reps):
            same = jnp.where(ids == doc, 1.0, 0.0)
            count = jnp.sum(jnp.sum(same, axis=0), axis=1, keepdims=True)
            length = length + same * count[None]
        weight[...] = jnp.sqrt(jnp.sqrt(tok / length))

    def column(slot, d):
        own = weight[d]
        mine = lax.broadcasted_iota(jnp.int32, own.shape, 0) == sec(-slot)
        line = jnp.sum(jnp.where(mine, own, 0.0), axis=0, keepdims=True)
        square = jnp.broadcast_to(line, (tok, tok))
        across_, along = [lax.broadcasted_iota(jnp.int32, (tok, tok), i) for i in (0, 1)]
        return jnp.sum(jnp.where(across_ == along, square, 0.0), axis=1, keepdims=True)

    back1, back2 = sec(-1), sec(-2)
    first1, _ = forward_spans(back1, n)
    first2, second2 = forward_spans(back2, n)
    strip = min(512, wide)

    def form(slot, d, place):
        scaled = column(slot, d)
        here = pl.ds(place * tok, tok)

        def fill(at, carry):
            on = pl.ds(pl.multiple_of(at * strip, strip), strip)
            act = buf[slot, d, :, on].astype(F32)
            if slot == 1:
                act = act + dot_nn(gbuf[0, d, :, 0:rank], upbuf[1, first1, :, on])
                act = act.astype(BF16).astype(F32)
            if slot == 2:
                act = act + dot_nn(gbuf[1, d, :, 0:rank], upbuf[2, first2, :, on])
                act = act.astype(BF16).astype(F32)
                act = act + dot_nn(gbuf[1, d, :, rank : 2 * rank], upbuf[1, second2, :, on])
                act = act.astype(BF16).astype(F32)
            rows[here, on] = (scaled * act).astype(BF16)
            return carry

        lax.fori_loop(0, wide // strip, fill, 0)

    def products(decay):
        offset = r * share % wide

        def one(at, carry):
            left = pl.multiple_of(offset + at * height, 128)
            right = pl.multiple_of(left // block * block, block)
            here = pl.ds(pl.multiple_of(at * height, height), height)
            gram = lax.dot_general(
                rows[:, pl.ds(left, height)], rows[:, pl.ds(right, block)], DOWNWARD,
                preferred_element_type=F32,
            )
            total[here] = decay * total[here] + gram * scale
            return carry

        lax.fori_loop(0, share // height, one, 0)

    held = {}
    g_copies, m_copies, c_copies = [], [], []
    span1, span2 = backward_span(s, 1, n), backward_span(s, 2, n)
    after = sec(1)

    def work0():
        own_chunk.wait()
        own_up.wait()
        w1_piece.wait_recv()
        held["w1"] = gather_start(0, fright.at[pl.ds(rank, rank), piece(r)])

    def work1():
        for load in forward_loads + backward_loads:
            load.wait()

    def work2():
        held["w1p"] = gather_pass(0, held["w1"])

    def work3():
        held["own3"] = keep(upbuf.at[2, span2, :, inner], bleft.at[pl.ds(2 * rank, rank), piece(r)])
        held["w3"] = gather_start(2, upbuf.at[2, span2, :, inner])
    def work4():
        held["w3p"] = gather_pass(2, held["w3"])
        gather_end(held["w1"], held["w1p"])
        both = long_dot(fleft, fright, tile)
        z = both[0:tok]
        g0 = (z / (1.0 + jnp.exp(-z)))[:, 0:rank].astype(BF16)
        later = lax.broadcasted_iota(jnp.int32, z.shape, 1) >= rank
        z = z + jnp.where(later, split_dot_right(g0, both[tok:]), 0.0)
        gsrc[...] = (z / (1.0 + jnp.exp(-z))).astype(BF16)
        for shift in (1, 2):
            for dc, e in slots:
                g_copies.append(
                    send(gsrc, gbuf.at[shift - 1, dc * 2 + e], sec(shift), rep(dc, e))
                )

    def work5():
        across["u", 0, 0].wait_recv()
        across["u", 1, 0].wait_recv()
        held["own2"] = keep(upbuf.at[1, span1, :, inner], bleft.at[pl.ds(rank, rank), piece(r)])
        held["w2"] = gather_start(1, upbuf.at[1, span1, :, inner])
        late2, late1 = backward_span(after, 2, n), backward_span(after, 1, n)
        first = keep(upbuf.at[1, late2, :, inner], msrc.at[0])
        second = keep(down.at[late1, :, piece(r)], msrc.at[1])
        first.wait()
        second.wait()
        mbuf[reps] = dot_nt(msrc[0], msrc[1])
        for dc, e in slots:
            m_copies.append(send(mbuf.at[reps], mbuf.at[dc * 2 + e], after, rep(dc, e)))

    def work6():
        held["w2p"] = gather_pass(1, held["w2"])

    def work7():
        gather_end(held["w3"], held["w3p"])
        gather_end(held["w2"], held["w2p"])
        held["own3"].wait()
        held["own2"].wait()
        both = long_dot(bleft, bright, tile)
        a0, a1, a2 = [both[i * rank : (i + 1) * rank, 0:tok] for i in range(3)]
        _, n1, n2 = [both[i * rank : (i + 1) * rank, tok : tok + rank] for i in range(3)]
        dz0 = (a0 * gate(stash_v[0])).astype(BF16)
        csrc[0] = dot_nt(dz0, dz0)
        a1 = a1 + split_dot_left(n1, dz0)
        st1.wait_recv()
        dz1 = (a1 * gate(stash_v[1])).astype(BF16)
        csrc[1] = dot_nt(dz1, dz1)
        for copy in m_copies:
            copy.wait_recv()
        n3 = mbuf[0]
        for d in range(1, reps):
            n3 = n3 + mbuf[d]
        a2 = a2 + split_dot_left(n2, dz0) + split_dot_left(n3, dz1)
        st2.wait_recv()
        dz2 = (a2 * gate(stash_v[2])).astype(BF16)
        csrc[2] = dot_nt(dz2, dz2)
        held["own_c"] = keep(csrc.at[0], cbuf.at[0, 0])
        for step in range(3):
            for dc, e in slots:
                if step == 0 and dc == 0 and e == 0:
                    continue
                c_copies.append(
                    send(csrc.at[step], cbuf.at[step, dc * 2 + e], sec(-step), rep(dc, e))
                )

    works = [work0, work1, work2, work3, work4, work5, work6, work7]
    started = set(range(2 * parts))

    def arrive(d):
        for at, (kind, of, _) in enumerate(pieces):
            if kind == "e" and of == d and at not in started:
                started.add(at)
                send_ahead(at)

    def own_products(start):
        for d in range(start, start + 4):
            form(0, d, d - start)
        products(0.75 if start == 0 else 1.0)

    waited = set()

    def wait_across(d):
        for b in range(parts):
            if (d, b) not in waited:
                waited.add((d, b))
                across["e", d, b].wait_recv()

    def relay(start):
        if start == 0:
            for copy in g_copies:
                copy.wait_recv()
        wait_across(start)
        wait_across(start + 1)
        for place, (slot, d) in enumerate([(1, start), (2, start), (1, start + 1), (2, start + 1)]):
            form(slot, d, place)
        products(1.0)

    for at in range(len(pieces)):
        if at == 1:
            arrive(1)
        if at == 3:
            for d in range(2, reps):
                arrive(d)
        ahead[at].wait_recv()
        if at == 0:
            works[0]()
        send_across(at)
        if 0 < at < len(works):
            works[at]()
        if at == 4:
            weigh()
            load_old.wait()
            own_products(0)
        if at == 8:
            relay(0)
    for start in range(4, reps, 4):
        own_products(start)
    for start in range(2, reps - 2, 2):
        relay(start)
    quarter = share // 4
    writes = [
        keep(total.at[pl.ds(i * quarter, quarter)], base.at[pl.ds(i * quarter, quarter)])
        for i in range(4)
    ]
    for d in (reps - 2, reps - 1):
        place = 2 * (d - reps + 2)
        wait_across(d)
        form(1, d, place)
        form(2, d, place + 1)
        done = pl.ds(place * tok, 2 * tok)
        writes.append(keep(rows.at[done], tail.at[done]))
    held["own_c"].wait()
    for copy in c_copies:
        copy.wait_recv()
    for write in writes:
        write.wait()
    for copy in copies:
        copy.wait_send()
    assert counts["copy"] <= send_sem.shape[0] and counts["local"] <= local_sem.shape[0]


def exchange(ent, ret, down, up, stash, docs, old, n, reps, wide, parts):
    tok, width = ent.shape
    rank = up.shape[1]
    slots = 140 if reps <= 4 else 60 * reps
    anywhere = pl.BlockSpec(memory_space=pltpu.HBM)
    return pl.pallas_call(
        functools.partial(exchange_kernel, n, reps, parts),
        out_shape=(
            jax.ShapeDtypeStruct(old.shape, F32),
            jax.ShapeDtypeStruct((4 * tok, wide), BF16),
            jax.ShapeDtypeStruct((3, reps, rank, rank), F32),
        ),
        in_specs=[anywhere] * 7,
        out_specs=(anywhere,) * 3,
        scratch_shapes=[
            pltpu.VMEM((3, reps, tok, wide), BF16),
            pltpu.VMEM((3, 2, rank, wide), BF16),
            pltpu.VMEM((2, reps, tok, 2 * rank), BF16),
            pltpu.VMEM((reps,) + docs.shape, jnp.int32),
            pltpu.VMEM((reps,) + docs.shape, F32),
            pltpu.VMEM((4 * tok, wide), BF16),
            pltpu.VMEM(old.shape, F32),
            pltpu.VMEM((tok + rank, width), BF16),
            pltpu.VMEM((2 * rank, width), BF16),
            pltpu.VMEM((3 * rank, width), BF16),
            pltpu.VMEM((tok + rank, width), BF16),
            pltpu.VMEM((3, rank, tok), F32),
            pltpu.VMEM((tok, 2 * rank), BF16),
            pltpu.VMEM((2, rank, width // reps), BF16),
            pltpu.VMEM((reps + 1, rank, rank), F32),
            pltpu.VMEM((3, rank, rank), F32),
            pltpu.SemaphoreType.DMA((32,)),
            pltpu.SemaphoreType.DMA((slots,)),
            pltpu.SemaphoreType.DMA((slots,)),
        ],
        compiler_params=pltpu.CompilerParams(
            collective_id=0, has_side_effects=True, vmem_limit_bytes=63 * 1024 * 1024
        ),
        name="exchange",
    )(ent, ret, down, up, stash, docs, old)


def factor_kernel(
    n, reps, base_rows, scale, tokens, upper, lower, cbuf, outer, base, base2, new, outer_new
):
    s = lax.axis_index("section")
    r = lax.axis_index("dp")
    step = pl.program_id(0)
    wide = upper.shape[1]
    height, block = new.shape
    share = base_rows
    inside = (r * share) % wide if share < wide else 0
    left = pl.multiple_of(inside + step * height, 128)
    right = pl.multiple_of(left // block * block, block)
    half = block // 2
    for at, old in enumerate((base, base2)):
        here = pl.ds(pl.multiple_of(right + at * half, 128), half)
        total = jnp.zeros((height, half), F32)
        for rows in (upper, lower):
            total = total + lax.dot_general(
                rows[:, pl.ds(left, height)], rows[:, here], DOWNWARD,
                preferred_element_type=F32,
            )
        new[:, at * half : (at + 1) * half] = old[...] + total * scale

    @pl.when(step == 0)
    def _():
        for span in range(2):
            sums = jnp.zeros(outer.shape[1:], F32)
            held = jnp.int32(0)
            for at in range(3):
                second = 1 - (s + at) // n
                member = second if span == 1 else 1 - second
                curv = cbuf[at, 0]
                for d in range(1, reps):
                    curv = curv + cbuf[at, d]
                sums = sums + jnp.where(member == 1, curv, 0.0)
                held = held + member
            divisor = jnp.maximum(held, 1).astype(F32) * tokens
            updated = 0.75 * outer[span] + 0.25 * sums / divisor
            outer_new[span] = jnp.where(held > 0, updated, outer[span])


def update_factor(rows, cbuf, outer, base, n, reps, tokens):
    share, block = base.shape
    height = min(256, share)
    whole = pl.BlockSpec(memory_space=pltpu.VMEM)
    tile = pl.BlockSpec((height, block), lambda i: (i, 0))
    return pl.pallas_call(
        functools.partial(factor_kernel, n, reps, share, 0.25 / (3 * tokens), tokens),
        out_shape=(
            jax.ShapeDtypeStruct(base.shape, F32), jax.ShapeDtypeStruct(outer.shape, F32)
        ),
        grid=(share // height,),
        in_specs=[
            pl.BlockSpec((rows.shape[0] // 2, rows.shape[1]), lambda i: (0, 0)),
            pl.BlockSpec((rows.shape[0] // 2, rows.shape[1]), lambda i: (1, 0)),
            whole, whole,
            pl.BlockSpec((height, block // 2), lambda i: (i, 0)),
            pl.BlockSpec((height, block // 2), lambda i: (i, 1)),
        ],
        out_specs=(tile, pl.BlockSpec(outer.shape, lambda i: (0, 0, 0))),
        compiler_params=pltpu.CompilerParams(vmem_limit_bytes=63 * 1024 * 1024),
        name="factor",
    )(rows, rows, cbuf, outer, base, base)


def shards(
    entering, returning, adapter_down, adapter_up, stashed, doc_ids, input_factor, output_factor
):
    n = lax.axis_size("section")
    reps = lax.axis_size("dp")
    tok, width = entering.shape[1:]
    block = input_factor.shape[2]
    wide = max(block, width // reps)
    base, tail, cbuf = exchange(
        entering[0], returning[0], adapter_down[:, 0], adapter_up[:, 0], stashed[0], doc_ids,
        input_factor[0], n, reps, wide, 2,
    )
    factor, outer = update_factor(tail, cbuf, output_factor[:, 0], base, n, reps, tok * reps)
    return factor[None], outer[:, None]


def solution(mesh):
    in_specs = (
        P("section", "dp", None),
        P("section", "dp", None),
        P(None, "section", None, None),
        P(None, "section", None, None),
        P("section", None, None, "dp"),
        P(None, "dp"),
        P("section", "dp", None),
        P(None, "section", None, None),
    )
    out_specs = (P("section", "dp", None), P(None, "section", None, None))
    return jax.shard_map(shards, mesh=mesh, in_specs=in_specs, out_specs=out_specs, check_vma=False)
```

```python
import functools

import jax
import jax.numpy as jnp
from jax import lax
from jax.experimental import pallas as pl
from jax.experimental.pallas import tpu as pltpu
from jax.sharding import PartitionSpec as P

BF16 = jnp.bfloat16
F32 = jnp.float32
ACROSS = (((1,), (1,)), ((), ()))
DOWNWARD = (((0,), (0,)), ((), ()))


def dot_nt(a, b):
    return lax.dot_general(a, b, ACROSS, preferred_element_type=F32)


def dot_nn(a, b):
    return jnp.dot(a, b, preferred_element_type=F32)


def long_dot(a_ref, b_ref, tile):
    width = a_ref.shape[-1]
    total = dot_nt(a_ref[:, 0:tile], b_ref[:, 0:tile])
    for at in range(tile, width, tile):
        total = total + dot_nt(a_ref[:, at : at + tile], b_ref[:, at : at + tile])
    return total


def split_dot_left(wide, narrow):
    high = wide.astype(BF16)
    low = (wide - high.astype(F32)).astype(BF16)
    return dot_nn(high, narrow) + dot_nn(low, narrow)


def split_dot_right(narrow, wide):
    high = wide.astype(BF16)
    low = (wide - high.astype(F32)).astype(BF16)
    return dot_nn(narrow, high) + dot_nn(narrow, low)


def forward_spans(anchor, n):
    first = 1 - anchor // (n // 2)
    return first, first + (anchor + 1) // n


def backward_span(anchor, step, n):
    section = (anchor - step + n) % n
    return 1 - (section + step) // n


def exchange_kernel(
    n, reps, parts,
    ent, ret, down, up, stash, docs, old,
    base, tail, cbuf,
    buf, upbuf, gbuf, docbuf, weight, rows, total,
    fleft, fright, bleft, bright, stash_v, gsrc, msrc, mbuf, csrc,
    local_sem, send_sem, recv_sem,
):
    s = lax.axis_index("section")
    r = lax.axis_index("dp")
    chips = reps // 2
    chip, core = r // 2, r % 2
    tok, width = ent.shape
    rank = up.shape[1]
    share = width // reps
    wide = buf.shape[-1]
    tile = min(2048, width)

    def sec(shift):
        return (s + shift + n) % n

    def rep(dc, e):
        return ((chip + dc + chips) % chips) * 2 + (core + e) % 2

    def cols(replica):
        return pl.ds(pl.multiple_of(replica * share // wide * wide, 128), wide)

    def piece(replica):
        return pl.ds(pl.multiple_of(replica * share, 128), share)

    inner = pl.ds(pl.multiple_of(r * share % wide, 128), share)
    slots = [(d // 2, d % 2) for d in range(reps)]
    counts = {"copy": 0, "local": 0}
    copies = []
    locals_ = []

    def send(src, dst, section, replica):
        at = counts["copy"]
        counts["copy"] += 1
        copy = pltpu.make_async_remote_copy(
            src_ref=src, dst_ref=dst, send_sem=send_sem.at[at], recv_sem=recv_sem.at[at],
            device_id=(section, replica), device_id_type=pl.DeviceIdType.MESH,
        )
        copy.start()
        copies.append(copy)
        return copy

    def keep(src, dst):
        at = counts["local"]
        counts["local"] += 1
        copy = pltpu.make_async_copy(src, dst, local_sem.at[at])
        copy.start()
        return copy

    c0, _ = forward_spans(s, n)
    forward_loads = [
        keep(ent, fleft.at[pl.ds(0, tok)]),
        keep(up.at[c0], fleft.at[pl.ds(tok, rank)]),
        keep(down.at[c0], fright.at[pl.ds(0, rank)]),
    ]
    backward_loads = [
        keep(ret, bright.at[pl.ds(0, tok)]),
        keep(down.at[1], bright.at[pl.ds(tok, rank)]),
        keep(up.at[1], bleft.at[pl.ds(0, rank)]),
        keep(stash.at[0], stash_v.at[0]),
    ]
    own_chunk = keep(ent.at[:, cols(r)], buf.at[0, 0])
    own_up = keep(up.at[:, :, cols(r)], upbuf.at[0])
    own_docs = keep(docs, docbuf.at[0])
    load_old = keep(old, total)

    barrier = pltpu.get_barrier_semaphore()
    peers = 0
    for shift in (0, 1, 2, -1, -2):
        for dc, e in slots:
            if shift == 0 and dc == 0 and e == 0:
                continue
            pl.semaphore_signal(
                barrier, inc=1, device_id=(sec(shift), rep(dc, e)),
                device_id_type=pl.DeviceIdType.MESH,
            )
            peers += 1
    pl.semaphore_wait(barrier, peers)

    half = tok // parts
    bands = [pl.ds(b * half, half) for b in range(parts)]
    pieces = [("e", 0, b) for b in range(parts)] + [("u", 0, 0), ("u", 1, 0)]
    pieces += [("e", d, b) for d in range(1, reps) for b in range(parts)]
    fulls = [
        (fright, pl.ds(rank, rank)), (bleft, pl.ds(rank, rank)), (bleft, pl.ds(2 * rank, rank))
    ]
    inside, ahead, across = {}, {}, {}
    arrived = set()
    odd = s % 2
    partner = s + 1 - 2 * odd

    def send_ahead(at):
        kind, d, b = pieces[at]
        if kind == "u":
            src, dst = upbuf.at[0, d], upbuf.at[2, d]
        else:
            dst = buf.at[2, d, bands[b]]
            if d == 0:
                src = fleft.at[bands[b], cols(r)]
            else:
                src = buf.at[0, d, bands[b]]
                if d not in arrived:
                    inside[slots[d]].wait_recv()
                    arrived.add(d)
        ahead[at] = send(src, dst, sec(2), r)

    def send_across(at):
        kind, d, b = pieces[at]
        if kind == "u":
            src, dst = upbuf.at[2 * odd, d], upbuf.at[1, d]
        else:
            src, dst = buf.at[2 * odd, d, bands[b]], buf.at[1, d, bands[b]]
        across[kind, d, b] = send(src, dst, partner, r)

    forward_loads[0].wait()
    own_up.wait()
    for at in range(2 * parts):
        send_ahead(at)
    prev = sec(-1)
    w1_piece = send(
        down.at[forward_spans(prev, n)[1], :, piece(r)], fright.at[pl.ds(rank, rank), piece(r)], prev, r
    )
    for dc, e in slots[1:]:
        target = rep(dc, e)
        inside[dc, e] = send(
            fleft.at[pl.ds(0, tok), cols(target)], buf.at[0, dc * 2 + e], s, target
        )
    doc_copies = [send(docs, docbuf.at[dc * 2 + e], s, rep(dc, e)) for dc, e in slots[1:]]
    st1 = send(stash.at[1], stash_v.at[1], sec(1), r)
    st2 = send(stash.at[2], stash_v.at[2], sec(2), r)

    def gather_start(which, own_ref):
        full, rows = fulls[which]
        mine = full.at[rows, piece(r)]
        out = {0: send(own_ref, mine, s, rep(0, 1))}
        for dc in range(1, chips):
            out[dc] = send(own_ref, mine, s, rep(dc, 0))
        return out

    def gather_pass(which, out):
        passed = []
        for dc in range(1, chips):
            out[dc].wait_recv()
            full, rows = fulls[which]
            theirs = full.at[rows, piece(rep(-dc, 0))]
            passed.append(send(theirs, theirs, s, rep(0, 1)))
        return passed

    def gather_end(out, passed):
        out[0].wait_recv()
        for copy in passed:
            copy.wait_recv()

    def gate(q):
        sigma = 1.0 / (1.0 + jnp.exp(-q))
        return sigma * (1.0 + q * (1.0 - sigma))

    block = total.shape[1]
    height = min(256, share)
    scale = 0.25 / (3 * tok * reps)

    def weigh():
        own_docs.wait()
        for copy in doc_copies:
            copy.wait_recv()
        ids = docbuf[...]
        length = jnp.zeros(ids.shape, F32)
        for doc in range(2 * reps):
            same = jnp.where(ids == doc, 1.0, 0.0)
            count = jnp.sum(jnp.sum(same, axis=0), axis=1, keepdims=True)
            length = length + same * count[None]
        weight[...] = jnp.sqrt(jnp.sqrt(tok / length))

    def column(slot, d):
        own = weight[d]
        mine = lax.broadcasted_iota(jnp.int32, own.shape, 0) == sec(-slot)
        line = jnp.sum(jnp.where(mine, own, 0.0), axis=0, keepdims=True)
        square = jnp.broadcast_to(line, (tok, tok))
        across_, along = [lax.broadcasted_iota(jnp.int32, (tok, tok), i) for i in (0, 1)]
        return jnp.sum(jnp.where(across_ == along, square, 0.0), axis=1, keepdims=True)

    back1, back2 = sec(-1), sec(-2)
    first1, _ = forward_spans(back1, n)
    first2, second2 = forward_spans(back2, n)
    strip = min(512, wide)

    def form(slot, d, place):
        scaled = column(slot, d)
        here = pl.ds(place * tok, tok)

        def fill(at, carry):
            on = pl.ds(pl.multiple_of(at * strip, strip), strip)
            act = buf[slot, d, :, on].astype(F32)
            if slot == 1:
                act = act + dot_nn(gbuf[0, d, :, 0:rank], upbuf[1, first1, :, on])
                act = act.astype(BF16).astype(F32)
            if slot == 2:
                act = act + dot_nn(gbuf[1, d, :, 0:rank], upbuf[2, first2, :, on])
                act = act.astype(BF16).astype(F32)
                act = act + dot_nn(gbuf[1, d, :, rank : 2 * rank], upbuf[1, second2, :, on])
                act = act.astype(BF16).astype(F32)
            rows[here, on] = (scaled * act).astype(BF16)
            return carry

        lax.fori_loop(0, wide // strip, fill, 0)

    def products(decay):
        offset = r * share % wide

        def one(at, carry):
            left = pl.multiple_of(offset + at * height, 128)
            right = pl.multiple_of(left // block * block, block)
            here = pl.ds(pl.multiple_of(at * height, height), height)
            gram = lax.dot_general(
                rows[:, pl.ds(left, height)], rows[:, pl.ds(right, block)], DOWNWARD,
                preferred_element_type=F32,
            )
            total[here] = decay * total[here] + gram * scale
            return carry

        lax.fori_loop(0, share // height, one, 0)

    held = {}
    g_copies, m_copies, c_copies = [], [], []
    span1, span2 = backward_span(s, 1, n), backward_span(s, 2, n)
    after = sec(1)

    def work0():
        own_chunk.wait()
        w1_piece.wait_recv()
        held["w1"] = gather_start(0, fright.at[pl.ds(rank, rank), piece(r)])

    def work1():
        for load in forward_loads[1:] + backward_loads:
            load.wait()

    def work2():
        held["w1p"] = gather_pass(0, held["w1"])

    def work3():
        held["own3"] = keep(upbuf.at[2, span2, :, inner], bleft.at[pl.ds(2 * rank, rank), piece(r)])
        held["w3"] = gather_start(2, upbuf.at[2, span2, :, inner])
    def work4():
        held["w3p"] = gather_pass(2, held["w3"])
        gather_end(held["w1"], held["w1p"])
        both = long_dot(fleft, fright, tile)
        z = both[0:tok]
        g0 = (z / (1.0 + jnp.exp(-z)))[:, 0:rank].astype(BF16)
        later = lax.broadcasted_iota(jnp.int32, z.shape, 1) >= rank
        z = z + jnp.where(later, split_dot_right(g0, both[tok:]), 0.0)
        gsrc[...] = (z / (1.0 + jnp.exp(-z))).astype(BF16)
        for shift in (1, 2):
            for dc, e in slots:
                g_copies.append(
                    send(gsrc, gbuf.at[shift - 1, dc * 2 + e], sec(shift), rep(dc, e))
                )

    def work5():
        across["u", 0, 0].wait_recv()
        across["u", 1, 0].wait_recv()
        held["own2"] = keep(upbuf.at[1, span1, :, inner], bleft.at[pl.ds(rank, rank), piece(r)])
        held["w2"] = gather_start(1, upbuf.at[1, span1, :, inner])
        late2, late1 = backward_span(after, 2, n), backward_span(after, 1, n)
        first = keep(upbuf.at[1, late2, :, inner], msrc.at[0])
        second = keep(down.at[late1, :, piece(r)], msrc.at[1])
        first.wait()
        second.wait()
        mbuf[reps] = dot_nt(msrc[0], msrc[1])
        for dc, e in slots:
            m_copies.append(send(mbuf.at[reps], mbuf.at[dc * 2 + e], after, rep(dc, e)))

    def work6():
        held["w2p"] = gather_pass(1, held["w2"])

    def work7():
        gather_end(held["w3"], held["w3p"])
        gather_end(held["w2"], held["w2p"])
        held["own3"].wait()
        held["own2"].wait()
        both = long_dot(bleft, bright, tile)
        a0, a1, a2 = [both[i * rank : (i + 1) * rank, 0:tok] for i in range(3)]
        _, n1, n2 = [both[i * rank : (i + 1) * rank, tok : tok + rank] for i in range(3)]
        dz0 = (a0 * gate(stash_v[0])).astype(BF16)
        csrc[0] = dot_nt(dz0, dz0)
        a1 = a1 + split_dot_left(n1, dz0)
        st1.wait_recv()
        dz1 = (a1 * gate(stash_v[1])).astype(BF16)
        csrc[1] = dot_nt(dz1, dz1)
        for copy in m_copies:
            copy.wait_recv()
        n3 = mbuf[0]
        for d in range(1, reps):
            n3 = n3 + mbuf[d]
        a2 = a2 + split_dot_left(n2, dz0) + split_dot_left(n3, dz1)
        st2.wait_recv()
        dz2 = (a2 * gate(stash_v[2])).astype(BF16)
        csrc[2] = dot_nt(dz2, dz2)
        held["own_c"] = keep(csrc.at[0], cbuf.at[0, 0])
        for step in range(3):
            for dc, e in slots:
                if step == 0 and dc == 0 and e == 0:
                    continue
                c_copies.append(
                    send(csrc.at[step], cbuf.at[step, dc * 2 + e], sec(-step), rep(dc, e))
                )

    works = [work0, work1, work2, work3, work4, work5, work6, work7]
    started = set(range(2 * parts))

    def arrive(d):
        for at, (kind, of, _) in enumerate(pieces):
            if kind == "e" and of == d and at not in started:
                started.add(at)
                send_ahead(at)

    def own_products(start):
        for d in range(start, start + 4):
            form(0, d, d - start)
        products(0.75 if start == 0 else 1.0)

    waited = set()

    def wait_across(d):
        for b in range(parts):
            if (d, b) not in waited:
                waited.add((d, b))
                across["e", d, b].wait_recv()

    def relay(start):
        if start == 0:
            for copy in g_copies:
                copy.wait_recv()
        wait_across(start)
        wait_across(start + 1)
        for place, (slot, d) in enumerate([(1, start), (2, start), (1, start + 1), (2, start + 1)]):
            form(slot, d, place)
        products(1.0)

    for at in range(len(pieces)):
        if at == 1:
            arrive(1)
        if at == 3:
            for d in range(2, reps):
                arrive(d)
        ahead[at].wait_recv()
        if at == 0:
            works[0]()
        send_across(at)
        if 0 < at < len(works):
            works[at]()
        if at == 4:
            weigh()
            load_old.wait()
            own_products(0)
        if at == 8:
            relay(0)
    for start in range(4, reps, 4):
        own_products(start)
    for start in range(2, reps - 2, 2):
        relay(start)
    quarter = share // 4
    writes = [
        keep(total.at[pl.ds(i * quarter, quarter)], base.at[pl.ds(i * quarter, quarter)])
        for i in range(4)
    ]
    for d in (reps - 2, reps - 1):
        place = 2 * (d - reps + 2)
        wait_across(d)
        form(1, d, place)
        form(2, d, place + 1)
        done = pl.ds(place * tok, 2 * tok)
        writes.append(keep(rows.at[done], tail.at[done]))
    held["own_c"].wait()
    for copy in c_copies:
        copy.wait_recv()
    for write in writes:
        write.wait()
    for copy in copies:
        copy.wait_send()
    assert counts["copy"] <= send_sem.shape[0] and counts["local"] <= local_sem.shape[0]


def exchange(ent, ret, down, up, stash, docs, old, n, reps, wide, parts):
    tok, width = ent.shape
    rank = up.shape[1]
    slots = 140 if reps <= 4 else 60 * reps
    anywhere = pl.BlockSpec(memory_space=pltpu.HBM)
    return pl.pallas_call(
        functools.partial(exchange_kernel, n, reps, parts),
        out_shape=(
            jax.ShapeDtypeStruct(old.shape, F32),
            jax.ShapeDtypeStruct((4 * tok, wide), BF16),
            jax.ShapeDtypeStruct((3, reps, rank, rank), F32),
        ),
        in_specs=[anywhere] * 7,
        out_specs=(anywhere,) * 3,
        scratch_shapes=[
            pltpu.VMEM((3, reps, tok, wide), BF16),
            pltpu.VMEM((3, 2, rank, wide), BF16),
            pltpu.VMEM((2, reps, tok, 2 * rank), BF16),
            pltpu.VMEM((reps,) + docs.shape, jnp.int32),
            pltpu.VMEM((reps,) + docs.shape, F32),
            pltpu.VMEM((4 * tok, wide), BF16),
            pltpu.VMEM(old.shape, F32),
            pltpu.VMEM((tok + rank, width), BF16),
            pltpu.VMEM((2 * rank, width), BF16),
            pltpu.VMEM((3 * rank, width), BF16),
            pltpu.VMEM((tok + rank, width), BF16),
            pltpu.VMEM((3, rank, tok), F32),
            pltpu.VMEM((tok, 2 * rank), BF16),
            pltpu.VMEM((2, rank, width // reps), BF16),
            pltpu.VMEM((reps + 1, rank, rank), F32),
            pltpu.VMEM((3, rank, rank), F32),
            pltpu.SemaphoreType.DMA((32,)),
            pltpu.SemaphoreType.DMA((slots,)),
            pltpu.SemaphoreType.DMA((slots,)),
        ],
        compiler_params=pltpu.CompilerParams(
            collective_id=0, has_side_effects=True, vmem_limit_bytes=63 * 1024 * 1024
        ),
        name="exchange",
    )(ent, ret, down, up, stash, docs, old)


def factor_kernel(
    n, reps, base_rows, scale, tokens, upper, lower, cbuf, outer, base, base2, new, outer_new
):
    s = lax.axis_index("section")
    r = lax.axis_index("dp")
    step = pl.program_id(0)
    wide = upper.shape[1]
    height, block = new.shape
    share = base_rows
    inside = (r * share) % wide if share < wide else 0
    left = pl.multiple_of(inside + step * height, 128)
    right = pl.multiple_of(left // block * block, block)
    half = block // 2
    for at, old in enumerate((base, base2)):
        here = pl.ds(pl.multiple_of(right + at * half, 128), half)
        total = jnp.zeros((height, half), F32)
        for rows in (upper, lower):
            total = total + lax.dot_general(
                rows[:, pl.ds(left, height)], rows[:, here], DOWNWARD,
                preferred_element_type=F32,
            )
        new[:, at * half : (at + 1) * half] = old[...] + total * scale

    @pl.when(step == 0)
    def _():
        for span in range(2):
            sums = jnp.zeros(outer.shape[1:], F32)
            held = jnp.int32(0)
            for at in range(3):
                second = 1 - (s + at) // n
                member = second if span == 1 else 1 - second
                curv = cbuf[at, 0]
                for d in range(1, reps):
                    curv = curv + cbuf[at, d]
                sums = sums + jnp.where(member == 1, curv, 0.0)
                held = held + member
            divisor = jnp.maximum(held, 1).astype(F32) * tokens
            updated = 0.75 * outer[span] + 0.25 * sums / divisor
            outer_new[span] = jnp.where(held > 0, updated, outer[span])


def update_factor(rows, cbuf, outer, base, n, reps, tokens):
    share, block = base.shape
    height = min(256, share)
    whole = pl.BlockSpec(memory_space=pltpu.VMEM)
    tile = pl.BlockSpec((height, block), lambda i: (i, 0))
    return pl.pallas_call(
        functools.partial(factor_kernel, n, reps, share, 0.25 / (3 * tokens), tokens),
        out_shape=(
            jax.ShapeDtypeStruct(base.shape, F32), jax.ShapeDtypeStruct(outer.shape, F32)
        ),
        grid=(share // height,),
        in_specs=[
            pl.BlockSpec((rows.shape[0] // 2, rows.shape[1]), lambda i: (0, 0)),
            pl.BlockSpec((rows.shape[0] // 2, rows.shape[1]), lambda i: (1, 0)),
            whole, whole,
            pl.BlockSpec((height, block // 2), lambda i: (i, 0)),
            pl.BlockSpec((height, block // 2), lambda i: (i, 1)),
        ],
        out_specs=(tile, pl.BlockSpec(outer.shape, lambda i: (0, 0, 0))),
        compiler_params=pltpu.CompilerParams(vmem_limit_bytes=63 * 1024 * 1024),
        name="factor",
    )(rows, rows, cbuf, outer, base, base)


def shards(
    entering, returning, adapter_down, adapter_up, stashed, doc_ids, input_factor, output_factor
):
    n = lax.axis_size("section")
    reps = lax.axis_size("dp")
    tok, width = entering.shape[1:]
    block = input_factor.shape[2]
    wide = max(block, width // reps)
    base, tail, cbuf = exchange(
        entering[0], returning[0], adapter_down[:, 0], adapter_up[:, 0], stashed[0], doc_ids,
        input_factor[0], n, reps, wide, 2,
    )
    factor, outer = update_factor(tail, cbuf, output_factor[:, 0], base, n, reps, tok * reps)
    return factor[None], outer[:, None]


def solution(mesh):
    in_specs = (
        P("section", "dp", None),
        P("section", "dp", None),
        P(None, "section", None, None),
        P(None, "section", None, None),
        P("section", None, None, "dp"),
        P(None, "dp"),
        P("section", "dp", None),
        P(None, "section", None, None),
    )
    out_specs = (P("section", "dp", None), P(None, "section", None, None))
    return jax.shard_map(shards, mesh=mesh, in_specs=in_specs, out_specs=out_specs, check_vma=False)
```

```python
import functools

import jax
import jax.numpy as jnp
from jax import lax
from jax.experimental import pallas as pl
from jax.experimental.pallas import tpu as pltpu
from jax.sharding import PartitionSpec as P

BF16 = jnp.bfloat16
F32 = jnp.float32
ACROSS = (((1,), (1,)), ((), ()))
DOWNWARD = (((0,), (0,)), ((), ()))


def dot_nt(a, b):
    return lax.dot_general(a, b, ACROSS, preferred_element_type=F32)


def dot_nn(a, b):
    return jnp.dot(a, b, preferred_element_type=F32)


def long_dot(a_ref, b_ref, tile):
    width = a_ref.shape[-1]
    total = dot_nt(a_ref[:, 0:tile], b_ref[:, 0:tile])
    for at in range(tile, width, tile):
        total = total + dot_nt(a_ref[:, at : at + tile], b_ref[:, at : at + tile])
    return total


def split_dot_left(wide, narrow):
    high = wide.astype(BF16)
    low = (wide - high.astype(F32)).astype(BF16)
    return dot_nn(high, narrow) + dot_nn(low, narrow)


def split_dot_right(narrow, wide):
    high = wide.astype(BF16)
    low = (wide - high.astype(F32)).astype(BF16)
    return dot_nn(narrow, high) + dot_nn(narrow, low)


def forward_spans(anchor, n):
    first = 1 - anchor // (n // 2)
    return first, first + (anchor + 1) // n


def backward_span(anchor, step, n):
    section = (anchor - step + n) % n
    return 1 - (section + step) // n


def exchange_kernel(
    n, reps, parts,
    ent, ret, down, up, stash, docs, old,
    base, tail, cbuf,
    buf, upbuf, gbuf, docbuf, weight, rows, total,
    fleft, fright, bleft, bright, stash_v, gsrc, msrc, mbuf, csrc,
    local_sem, send_sem, recv_sem,
):
    s = lax.axis_index("section")
    r = lax.axis_index("dp")
    chips = reps // 2
    chip, core = r // 2, r % 2
    tok, width = ent.shape
    rank = up.shape[1]
    share = width // reps
    wide = buf.shape[-1]
    tile = min(2048, width)

    def sec(shift):
        return (s + shift + n) % n

    def rep(dc, e):
        return ((chip + dc + chips) % chips) * 2 + (core + e) % 2

    def cols(replica):
        return pl.ds(pl.multiple_of(replica * share // wide * wide, 128), wide)

    def piece(replica):
        return pl.ds(pl.multiple_of(replica * share, 128), share)

    inner = pl.ds(pl.multiple_of(r * share % wide, 128), share)
    slots = [(d // 2, d % 2) for d in range(reps)]
    counts = {"copy": 0, "local": 0}
    copies = []
    locals_ = []

    def send(src, dst, section, replica):
        at = counts["copy"]
        counts["copy"] += 1
        copy = pltpu.make_async_remote_copy(
            src_ref=src, dst_ref=dst, send_sem=send_sem.at[at], recv_sem=recv_sem.at[at],
            device_id=(section, replica), device_id_type=pl.DeviceIdType.MESH,
        )
        copy.start()
        copies.append(copy)
        return copy

    def keep(src, dst):
        at = counts["local"]
        counts["local"] += 1
        copy = pltpu.make_async_copy(src, dst, local_sem.at[at])
        copy.start()
        return copy

    c0, _ = forward_spans(s, n)
    forward_loads = [
        keep(ent, fleft.at[pl.ds(0, tok)]),
        keep(up.at[c0], fleft.at[pl.ds(tok, rank)]),
        keep(down.at[c0], fright.at[pl.ds(0, rank)]),
    ]
    backward_loads = [
        keep(ret, bright.at[pl.ds(0, tok)]),
        keep(down.at[1], bright.at[pl.ds(tok, rank)]),
        keep(up.at[1], bleft.at[pl.ds(0, rank)]),
        keep(stash.at[0], stash_v.at[0]),
    ]
    own_chunk = keep(ent.at[:, cols(r)], buf.at[0, 0])
    own_up = keep(up.at[:, :, cols(r)], upbuf.at[0])
    own_docs = keep(docs, docbuf.at[0])
    load_old = keep(old, total)

    barrier = pltpu.get_barrier_semaphore()
    peers = 0
    for shift in (0, 1, 2, -1, -2):
        for dc, e in slots:
            if shift == 0 and dc == 0 and e == 0:
                continue
            pl.semaphore_signal(
                barrier, inc=1, device_id=(sec(shift), rep(dc, e)),
                device_id_type=pl.DeviceIdType.MESH,
            )
            peers += 1
    pl.semaphore_wait(barrier, peers)

    half = tok // parts
    bands = [pl.ds(b * half, half) for b in range(parts)]
    pieces = [("e", 0, b) for b in range(parts)] + [("u", 0, 0), ("u", 1, 0)]
    pieces += [("e", d, b) for d in range(1, reps) for b in range(parts)]
    fulls = [
        (fright, pl.ds(rank, rank)), (bleft, pl.ds(rank, rank)), (bleft, pl.ds(2 * rank, rank))
    ]
    inside, ahead, across = {}, {}, {}
    arrived = set()
    odd = s % 2
    partner = s + 1 - 2 * odd

    def send_ahead(at):
        kind, d, b = pieces[at]
        if kind == "u":
            src, dst = upbuf.at[0, d], upbuf.at[2, d]
        else:
            dst = buf.at[2, d, bands[b]]
            if d == 0:
                src = fleft.at[bands[b], cols(r)]
            else:
                src = buf.at[0, d, bands[b]]
                if d not in arrived:
                    inside[slots[d]].wait_recv()
                    arrived.add(d)
        ahead[at] = send(src, dst, sec(2), r)

    def send_across(at):
        kind, d, b = pieces[at]
        if kind == "u":
            src, dst = upbuf.at[2 * odd, d], upbuf.at[1, d]
        else:
            src, dst = buf.at[2 * odd, d, bands[b]], buf.at[1, d, bands[b]]
        across[kind, d, b] = send(src, dst, partner, r)

    forward_loads[0].wait()
    own_up.wait()
    for at in range(2 * parts):
        send_ahead(at)
    prev = sec(-1)
    w1_piece = send(
        down.at[forward_spans(prev, n)[1], :, piece(r)], fright.at[pl.ds(rank, rank), piece(r)], prev, r
    )
    for dc, e in slots[1:]:
        target = rep(dc, e)
        inside[dc, e] = send(
            fleft.at[pl.ds(0, tok), cols(target)], buf.at[0, dc * 2 + e], s, target
        )
    doc_copies = [send(docs, docbuf.at[dc * 2 + e], s, rep(dc, e)) for dc, e in slots[1:]]
    st1 = send(stash.at[1], stash_v.at[1], sec(1), r)
    st2 = send(stash.at[2], stash_v.at[2], sec(2), r)

    def gather_start(which, own_ref):
        full, rows = fulls[which]
        mine = full.at[rows, piece(r)]
        out = {0: send(own_ref, mine, s, rep(0, 1))}
        for dc in range(1, chips):
            out[dc] = send(own_ref, mine, s, rep(dc, 0))
        return out

    def gather_pass(which, out):
        passed = []
        for dc in range(1, chips):
            out[dc].wait_recv()
            full, rows = fulls[which]
            theirs = full.at[rows, piece(rep(-dc, 0))]
            passed.append(send(theirs, theirs, s, rep(0, 1)))
        return passed

    def gather_end(out, passed):
        out[0].wait_recv()
        for copy in passed:
            copy.wait_recv()

    def gate(q):
        sigma = 1.0 / (1.0 + jnp.exp(-q))
        return sigma * (1.0 + q * (1.0 - sigma))

    block = total.shape[1]
    height = min(256, share)
    scale = 0.25 / (3 * tok * reps)

    def weigh():
        own_docs.wait()
        for copy in doc_copies:
            copy.wait_recv()
        ids = docbuf[...]
        length = jnp.zeros(ids.shape, F32)
        for doc in range(2 * reps):
            same = jnp.where(ids == doc, 1.0, 0.0)
            count = jnp.sum(jnp.sum(same, axis=0), axis=1, keepdims=True)
            length = length + same * count[None]
        weight[...] = jnp.sqrt(jnp.sqrt(tok / length))

    def column(slot, d):
        own = weight[d]
        mine = lax.broadcasted_iota(jnp.int32, own.shape, 0) == sec(-slot)
        line = jnp.sum(jnp.where(mine, own, 0.0), axis=0, keepdims=True)
        square = jnp.broadcast_to(line, (tok, tok))
        across_, along = [lax.broadcasted_iota(jnp.int32, (tok, tok), i) for i in (0, 1)]
        return jnp.sum(jnp.where(across_ == along, square, 0.0), axis=1, keepdims=True)

    back1, back2 = sec(-1), sec(-2)
    first1, _ = forward_spans(back1, n)
    first2, second2 = forward_spans(back2, n)
    strip = min(512, wide)

    def form(slot, d, place):
        scaled = column(slot, d)
        here = pl.ds(place * tok, tok)

        def fill(at, carry):
            on = pl.ds(pl.multiple_of(at * strip, strip), strip)
            act = buf[slot, d, :, on].astype(F32)
            if slot == 1:
                act = act + dot_nn(gbuf[0, d, :, 0:rank], upbuf[1, first1, :, on])
                act = act.astype(BF16).astype(F32)
            if slot == 2:
                act = act + dot_nn(gbuf[1, d, :, 0:rank], upbuf[2, first2, :, on])
                act = act.astype(BF16).astype(F32)
                act = act + dot_nn(gbuf[1, d, :, rank : 2 * rank], upbuf[1, second2, :, on])
                act = act.astype(BF16).astype(F32)
            rows[here, on] = (scaled * act).astype(BF16)
            return carry

        lax.fori_loop(0, wide // strip, fill, 0)

    def products(decay):
        offset = r * share % wide

        def one(at, carry):
            left = pl.multiple_of(offset + at * height, 128)
            right = pl.multiple_of(left // block * block, block)
            here = pl.ds(pl.multiple_of(at * height, height), height)
            gram = lax.dot_general(
                rows[:, pl.ds(left, height)], rows[:, pl.ds(right, block)], DOWNWARD,
                preferred_element_type=F32,
            )
            total[here] = decay * total[here] + gram * scale
            return carry

        lax.fori_loop(0, share // height, one, 0)

    held = {}
    g_copies, m_copies, c_copies = [], [], []
    span1, span2 = backward_span(s, 1, n), backward_span(s, 2, n)
    after = sec(1)

    def work0():
        own_chunk.wait()
        w1_piece.wait_recv()
        held["w1"] = gather_start(0, fright.at[pl.ds(rank, rank), piece(r)])

    def work1():
        for load in forward_loads[1:] + backward_loads:
            load.wait()

    def work2():
        held["w1p"] = gather_pass(0, held["w1"])

    def work3():
        held["own3"] = keep(upbuf.at[2, span2, :, inner], bleft.at[pl.ds(2 * rank, rank), piece(r)])
        held["w3"] = gather_start(2, upbuf.at[2, span2, :, inner])
    def work4():
        held["w3p"] = gather_pass(2, held["w3"])
        gather_end(held["w1"], held["w1p"])
        both = long_dot(fleft, fright, tile)
        z = both[0:tok]
        g0 = (z / (1.0 + jnp.exp(-z)))[:, 0:rank].astype(BF16)
        later = lax.broadcasted_iota(jnp.int32, z.shape, 1) >= rank
        z = z + jnp.where(later, split_dot_right(g0, both[tok:]), 0.0)
        gsrc[...] = (z / (1.0 + jnp.exp(-z))).astype(BF16)
        for shift in (1, 2):
            for dc, e in slots:
                g_copies.append(
                    send(gsrc, gbuf.at[shift - 1, dc * 2 + e], sec(shift), rep(dc, e))
                )

    def work5():
        across["u", 0, 0].wait_recv()
        across["u", 1, 0].wait_recv()
        held["own2"] = keep(upbuf.at[1, span1, :, inner], bleft.at[pl.ds(rank, rank), piece(r)])
        held["w2"] = gather_start(1, upbuf.at[1, span1, :, inner])
        late2, late1 = backward_span(after, 2, n), backward_span(after, 1, n)
        first = keep(upbuf.at[1, late2, :, inner], msrc.at[0])
        second = keep(down.at[late1, :, piece(r)], msrc.at[1])
        first.wait()
        second.wait()
        mbuf[reps] = dot_nt(msrc[0], msrc[1])
        for dc, e in slots:
            m_copies.append(send(mbuf.at[reps], mbuf.at[dc * 2 + e], after, rep(dc, e)))

    def work6():
        held["w2p"] = gather_pass(1, held["w2"])

    def work7():
        gather_end(held["w3"], held["w3p"])
        gather_end(held["w2"], held["w2p"])
        held["own3"].wait()
        held["own2"].wait()
        both = long_dot(bleft, bright, tile)
        a0, a1, a2 = [both[i * rank : (i + 1) * rank, 0:tok] for i in range(3)]
        _, n1, n2 = [both[i * rank : (i + 1) * rank, tok : tok + rank] for i in range(3)]
        dz0 = (a0 * gate(stash_v[0])).astype(BF16)
        csrc[0] = dot_nt(dz0, dz0)
        a1 = a1 + split_dot_left(n1, dz0)
        st1.wait_recv()
        dz1 = (a1 * gate(stash_v[1])).astype(BF16)
        csrc[1] = dot_nt(dz1, dz1)
        for copy in m_copies:
            copy.wait_recv()
        n3 = mbuf[0]
        for d in range(1, reps):
            n3 = n3 + mbuf[d]
        a2 = a2 + split_dot_left(n2, dz0) + split_dot_left(n3, dz1)
        st2.wait_recv()
        dz2 = (a2 * gate(stash_v[2])).astype(BF16)
        csrc[2] = dot_nt(dz2, dz2)
        held["own_c"] = keep(csrc.at[0], cbuf.at[0, 0])
        for step in range(3):
            for dc, e in slots:
                if step == 0 and dc == 0 and e == 0:
                    continue
                c_copies.append(
                    send(csrc.at[step], cbuf.at[step, dc * 2 + e], sec(-step), rep(dc, e))
                )

    works = [work0, work1, work2, work3, work4, work5, work6, work7]
    started = set(range(2 * parts))

    def arrive(d):
        for at, (kind, of, _) in enumerate(pieces):
            if kind == "e" and of == d and at not in started:
                started.add(at)
                send_ahead(at)

    def own_products(start):
        for d in range(start, start + 4):
            form(0, d, d - start)
        products(0.75 if start == 0 else 1.0)

    waited = set()

    def wait_across(d):
        for b in range(parts):
            if (d, b) not in waited:
                waited.add((d, b))
                across["e", d, b].wait_recv()

    def relay(start):
        if start == 0:
            for copy in g_copies:
                copy.wait_recv()
        wait_across(start)
        wait_across(start + 1)
        for place, (slot, d) in enumerate([(1, start), (2, start), (1, start + 1), (2, start + 1)]):
            form(slot, d, place)
        products(1.0)

    for at in range(len(pieces)):
        if at == 1:
            arrive(1)
        if at == 3:
            for d in range(2, reps):
                arrive(d)
        ahead[at].wait_recv()
        if at == 0:
            works[0]()
        send_across(at)
        if 0 < at < len(works):
            works[at]()
        if at == 4:
            weigh()
            load_old.wait()
            own_products(0)
        if at == 8:
            relay(0)
    for start in range(4, reps, 4):
        own_products(start)
    for start in range(2, reps - 2, 2):
        relay(start)
    quarter = share // 4
    writes = [
        keep(total.at[pl.ds(i * quarter, quarter)], base.at[pl.ds(i * quarter, quarter)])
        for i in range(4)
    ]
    for d in (reps - 2, reps - 1):
        place = 2 * (d - reps + 2)
        wait_across(d)
        form(1, d, place)
        form(2, d, place + 1)
        done = pl.ds(place * tok, 2 * tok)
        writes.append(keep(rows.at[done], tail.at[done]))
    held["own_c"].wait()
    for copy in c_copies:
        copy.wait_recv()
    for write in writes:
        write.wait()
    for copy in copies:
        copy.wait_send()
    assert counts["copy"] <= send_sem.shape[0] and counts["local"] <= local_sem.shape[0]


def exchange(ent, ret, down, up, stash, docs, old, n, reps, wide, parts):
    tok, width = ent.shape
    rank = up.shape[1]
    slots = 140 if reps <= 4 else 60 * reps
    anywhere = pl.BlockSpec(memory_space=pltpu.HBM)
    return pl.pallas_call(
        functools.partial(exchange_kernel, n, reps, parts),
        out_shape=(
            jax.ShapeDtypeStruct(old.shape, F32),
            jax.ShapeDtypeStruct((4 * tok, wide), BF16),
            jax.ShapeDtypeStruct((3, reps, rank, rank), F32),
        ),
        in_specs=[anywhere] * 7,
        out_specs=(anywhere,) * 3,
        scratch_shapes=[
            pltpu.VMEM((3, reps, tok, wide), BF16),
            pltpu.VMEM((3, 2, rank, wide), BF16),
            pltpu.VMEM((2, reps, tok, 2 * rank), BF16),
            pltpu.VMEM((reps,) + docs.shape, jnp.int32),
            pltpu.VMEM((reps,) + docs.shape, F32),
            pltpu.VMEM((4 * tok, wide), BF16),
            pltpu.VMEM(old.shape, F32),
            pltpu.VMEM((tok + rank, width), BF16),
            pltpu.VMEM((2 * rank, width), BF16),
            pltpu.VMEM((3 * rank, width), BF16),
            pltpu.VMEM((tok + rank, width), BF16),
            pltpu.VMEM((3, rank, tok), F32),
            pltpu.VMEM((tok, 2 * rank), BF16),
            pltpu.VMEM((2, rank, width // reps), BF16),
            pltpu.VMEM((reps + 1, rank, rank), F32),
            pltpu.VMEM((3, rank, rank), F32),
            pltpu.SemaphoreType.DMA((32,)),
            pltpu.SemaphoreType.DMA((slots,)),
            pltpu.SemaphoreType.DMA((slots,)),
        ],
        compiler_params=pltpu.CompilerParams(
            collective_id=0, has_side_effects=True, vmem_limit_bytes=63 * 1024 * 1024
        ),
        name="exchange",
    )(ent, ret, down, up, stash, docs, old)


def factor_kernel(
    n, reps, base_rows, scale, tokens, upper, lower, cbuf, outer, base, base2, new, outer_new
):
    s = lax.axis_index("section")
    r = lax.axis_index("dp")
    step = pl.program_id(0)
    wide = upper.shape[1]
    height, block = new.shape
    share = base_rows
    inside = (r * share) % wide if share < wide else 0
    left = pl.multiple_of(inside + step * height, 128)
    right = pl.multiple_of(left // block * block, block)
    half = block // 2
    for at, old in enumerate((base, base2)):
        here = pl.ds(pl.multiple_of(right + at * half, 128), half)
        total = jnp.zeros((height, half), F32)
        for rows in (upper, lower):
            total = total + lax.dot_general(
                rows[:, pl.ds(left, height)], rows[:, here], DOWNWARD,
                preferred_element_type=F32,
            )
        new[:, at * half : (at + 1) * half] = old[...] + total * scale

    @pl.when(step == 0)
    def _():
        for span in range(2):
            sums = jnp.zeros(outer.shape[1:], F32)
            held = jnp.int32(0)
            for at in range(3):
                second = 1 - (s + at) // n
                member = second if span == 1 else 1 - second
                curv = cbuf[at, 0]
                for d in range(1, reps):
                    curv = curv + cbuf[at, d]
                sums = sums + jnp.where(member == 1, curv, 0.0)
                held = held + member
            divisor = jnp.maximum(held, 1).astype(F32) * tokens
            updated = 0.75 * outer[span] + 0.25 * sums / divisor
            outer_new[span] = jnp.where(held > 0, updated, outer[span])


def update_factor(rows, cbuf, outer, base, n, reps, tokens):
    share, block = base.shape
    height = min(512, share)
    whole = pl.BlockSpec(memory_space=pltpu.VMEM)
    tile = pl.BlockSpec((height, block), lambda i: (i, 0))
    return pl.pallas_call(
        functools.partial(factor_kernel, n, reps, share, 0.25 / (3 * tokens), tokens),
        out_shape=(
            jax.ShapeDtypeStruct(base.shape, F32), jax.ShapeDtypeStruct(outer.shape, F32)
        ),
        grid=(share // height,),
        in_specs=[
            pl.BlockSpec((rows.shape[0] // 2, rows.shape[1]), lambda i: (0, 0)),
            pl.BlockSpec((rows.shape[0] // 2, rows.shape[1]), lambda i: (1, 0)),
            whole, whole,
            pl.BlockSpec((height, block // 2), lambda i: (i, 0)),
            pl.BlockSpec((height, block // 2), lambda i: (i, 1)),
        ],
        out_specs=(tile, pl.BlockSpec(outer.shape, lambda i: (0, 0, 0))),
        compiler_params=pltpu.CompilerParams(vmem_limit_bytes=63 * 1024 * 1024),
        name="factor",
    )(rows, rows, cbuf, outer, base, base)


def shards(
    entering, returning, adapter_down, adapter_up, stashed, doc_ids, input_factor, output_factor
):
    n = lax.axis_size("section")
    reps = lax.axis_size("dp")
    tok, width = entering.shape[1:]
    block = input_factor.shape[2]
    wide = max(block, width // reps)
    base, tail, cbuf = exchange(
        entering[0], returning[0], adapter_down[:, 0], adapter_up[:, 0], stashed[0], doc_ids,
        input_factor[0], n, reps, wide, 2,
    )
    factor, outer = update_factor(tail, cbuf, output_factor[:, 0], base, n, reps, tok * reps)
    return factor[None], outer[:, None]


def solution(mesh):
    in_specs = (
        P("section", "dp", None),
        P("section", "dp", None),
        P(None, "section", None, None),
        P(None, "section", None, None),
        P("section", None, None, "dp"),
        P(None, "dp"),
        P("section", "dp", None),
        P(None, "section", None, None),
    )
    out_specs = (P("section", "dp", None), P(None, "section", None, None))
    return jax.shard_map(shards, mesh=mesh, in_specs=in_specs, out_specs=out_specs, check_vma=False)
```
